128 devices in a mesh: gx: 16 (over z_hi, x, core), gy: 8 (over z_lo, y).
Axes of the slice: x: 4, y: 4, z: 4 (z_hi: 2, z_lo: 2; z = z_hi * 2 + z_lo), core: 2. Of those that a mesh axis runs over, the one named last changes fastest.
Arguments:
- state: float32 [64, 8, 256, 1024], P(None, None, 'gx', 'gy'), may hold values from -6 to 6
- east_wind: float32 [64, 256, 1024], P(None, 'gx', 'gy'), may hold values from -0.24 to 0.24
- north_wind: float32 [64, 256, 1024], P(None, 'gx', 'gy'), may hold values from -0.24 to 0.24
- kappa: float32 [63, 256, 1024], P(None, 'gx', 'gy'), may hold values from 0.05 to 500
- w_in: bfloat16 [256, 512], replicated, may hold values from -0.375 to 0.375
- w_mid: bfloat16 [512, 512], replicated, may hold values from -0.25 to 0.25
- w_out: bfloat16 [512, 256], replicated, may hold values from -0.25 to 0.25
- cotangent: bfloat16 [262144, 256], P(('gx', 'gy')), may hold values from -6 to 6
Outputs:
- new_state: float32 [64, 8, 256, 1024], P(None, None, 'gx', 'gy')
- adjoint: bfloat16 [262144, 256], P(('gx', 'gy'))
The draws below stay inside these ranges and needn't reach their ends.
All inputs are finite; a program needn't handle non-finite values.
Results may differ from the reference program's by a relative error of at most 0.006.
The reference program's roundings to bfloat16 on the way (of `inputs`, `act_one`, `act_two`, `tend`, `delta_two` and `delta_one`) count: a program that leaves them out, or rounds other values in their place, can miss the bound.
Values may be sent and summed in bfloat16 or wider, within the bound.
No kernel may reach another device: no remote copies, remote signals or barrier semaphores. Data moves between devices by JAX's collectives and lax.ppermute only.
A program may use at most 128 MiB of HBM per device.

```python
import math
import jax
import jax.numpy as jnp
from jax import lax

LEVELS = 64
FIELDS = 8
PHYS_FIELDS = 4
HIDDEN_SIZE = 512
FEATURES = 256
CX = 16
CY = 128
NX = 256
NY = 1024
COLUMNS = 262144
N_GX = 16
N_GY = 8


def draw_state(key, part):
    key = jax.random.fold_in(key, 11)
    key_base, key_slope, key_noise = jax.random.split(key, 3)
    level = jnp.arange(LEVELS, dtype=jnp.float32)
    ramp = (2.0 * level / max(LEVELS - 1, 1) - 1.0).reshape(LEVELS, 1, 1, 1)
    base = jnp.clip(jax.random.normal(key_base, (FIELDS, NX, NY), jnp.float32), -2.0, 2.0)
    slope = jax.random.uniform(key_slope, (FIELDS, NX, NY), jnp.float32, -1.5, 1.5)
    noise = 0.5 * jnp.clip(jax.random.normal(key_noise, (LEVELS, FIELDS, NX, NY), jnp.float32), -3.0, 3.0)
    return (base[None] + slope[None] * ramp + noise).astype(jnp.float32)


def draw_kappa(key, part):
    key = jax.random.fold_in(key, 23)
    key_one, key_two = jax.random.split(key, 2)
    low_log = math.log(0.05)
    high_log = math.log(250.0)
    base = jnp.exp(jax.random.uniform(key_one, (NX, NY), jnp.float32, low_log, high_log))
    factor = jnp.exp(jax.random.uniform(key_two, (LEVELS - 1, NX, NY), jnp.float32, 0.0, math.log(2.0)))
    return jnp.clip(base[None] * factor, 0.05, 500.0).astype(jnp.float32)


def level_of(stream_key, shape, cuts, low, largest):
    def one(dim, blocks):
        heights = jax.random.uniform(jax.random.fold_in(jax.random.fold_in(stream_key, 6), dim), (blocks,), jnp.float32, low / len(cuts), largest / len(cuts))
        return jnp.repeat(jnp.exp(heights), shape[dim] // blocks).reshape((-1,) + (1,) * (len(shape) - dim - 1))

    factor_of = one(*cuts[0])
    for cut in cuts[1:]:
        factor_of = factor_of * one(*cut)
    return factor_of


def scatter_about(rng, dims, deviation, limit, cuts=(), kind=jnp.bfloat16):
    values = jax.random.normal(rng, dims, jnp.float32) * deviation
    if len(cuts) > 0:
        values = level_of(rng, dims, cuts, -0.22, 0.18) * values
    return jnp.clip(values, min=-limit, max=limit).astype(kind)


def setup_inputs(seed: int = 0) -> dict:
    seeds = jax.random.split(jax.random.key(seed), 9)
    state = draw_state(jax.random.fold_in(seeds[8], 71), 0)
    east_wind = jnp.clip(jax.random.uniform(seeds[1], (LEVELS, NX, NY), jnp.float32, -0.24, 0.24) * level_of(seeds[1], (LEVELS, NX, NY), ((1, 16), (2, 8)), -0.4, 0.0), -0.24, 0.24)
    north_wind = jnp.clip(jax.random.uniform(seeds[2], (LEVELS, NX, NY), jnp.float32, -0.24, 0.24) * level_of(seeds[2], (LEVELS, NX, NY), ((1, 16), (2, 8)), -0.4, 0.0), -0.24, 0.24)
    kappa = draw_kappa(jax.random.fold_in(seeds[8], 71), 0)
    w_in = scatter_about(seeds[4], (FEATURES, HIDDEN_SIZE), FEATURES ** -0.5, 0.375)
    w_mid = scatter_about(seeds[5], (HIDDEN_SIZE, HIDDEN_SIZE), HIDDEN_SIZE ** -0.5, 0.25)
    w_out = scatter_about(seeds[6], (HIDDEN_SIZE, FEATURES), HIDDEN_SIZE ** -0.5, 0.25)
    cotangent = scatter_about(seeds[7], (COLUMNS, FEATURES), 1.0, 6.0, ((0, 128),))
    return {"state": state, "east_wind": east_wind, "north_wind": north_wind, "kappa": kappa, "w_in": w_in, "w_mid": w_mid, "w_out": w_out, "cotangent": cotangent}


def upwind_step(tracer, east_speed, north_speed):
    east_speed = east_speed[..., None, :, :]
    north_speed = north_speed[..., None, :, :]
    east_rate = east_speed[..., :-1, 1:-1]
    flux_east = jnp.maximum(east_rate, 0.0) * tracer[..., :-1, 1:-1] + jnp.minimum(east_rate, 0.0) * tracer[..., 1:, 1:-1]
    north_rate = north_speed[..., 1:-1, :-1]
    flux_north = jnp.maximum(north_rate, 0.0) * tracer[..., 1:-1, :-1] + jnp.minimum(north_rate, 0.0) * tracer[..., 1:-1, 1:]
    return tracer[..., 1:-1, 1:-1] - (flux_east[..., 1:, :] - flux_east[..., :-1, :]) - (flux_north[..., :, 1:] - flux_north[..., :, :-1])


def diffuse(field, kappa):
    edge_row = jnp.zeros_like(kappa[:1])
    coupling = jnp.concatenate([edge_row, kappa, edge_row], axis=0)

    def downward(state_carry, entries):
        factor_prev, rhs_prev = state_carry
        below_coef, above_coef, source = entries
        pivot_value = 1.0 + below_coef + above_coef - below_coef * factor_prev
        factor_next = above_coef / pivot_value
        rhs_next = (source + below_coef[None] * rhs_prev) / pivot_value[None]
        return (factor_next, rhs_next), (factor_next, rhs_next)

    initial = (jnp.zeros_like(kappa[0]), jnp.zeros_like(field[0]))
    _, (factors, rhs_all) = lax.scan(downward, initial, (coupling[:-1], coupling[1:], field))

    def upward(above_level, entries):
        factor, rhs_level = entries
        solved_level = rhs_level + factor[None] * above_level
        return solved_level, solved_level

    _, solved = lax.scan(upward, jnp.zeros_like(field[0]), (factors, rhs_all), reverse=True)
    return solved


def silu_slope(values):
    sigma = jax.nn.sigmoid(values)
    return sigma * (1.0 + values * (1.0 - sigma))


def contract_last(left, right):
    return lax.dot_general(left, right, (((1,), (1,)), ((), ())), preferred_element_type=jnp.float32)


def physics(inputs, cotan, w_in, w_mid, w_out):
    first = jnp.dot(inputs, w_in, preferred_element_type=jnp.float32)
    act_one = jax.nn.silu(first).astype(jnp.bfloat16)
    second = jnp.dot(act_one, w_mid, preferred_element_type=jnp.float32)
    act_two = jax.nn.silu(second).astype(jnp.bfloat16)
    tend = jnp.dot(act_two, w_out, preferred_element_type=jnp.float32).astype(jnp.bfloat16)
    delta_two = (contract_last(cotan, w_out) * silu_slope(second)).astype(jnp.bfloat16)
    delta_one = (contract_last(delta_two, w_mid) * silu_slope(first)).astype(jnp.bfloat16)
    adjoint = contract_last(delta_one, w_in).astype(jnp.bfloat16)
    return tend, adjoint


def reference(state, east_wind, north_wind, kappa, w_in, w_mid, w_out, cotangent):
    def advect(entries):
        tracer, east_speed, north_speed = entries
        east_speed = east_speed.at[-1, :].set(0.0)
        north_speed = north_speed.at[:, -1].set(0.0)
        east_pad = jnp.pad(east_speed, 1)
        north_pad = jnp.pad(north_speed, 1)
        first_pass = upwind_step(jnp.pad(tracer, ((0, 0), (1, 1), (1, 1))), east_pad, north_pad)
        return upwind_step(jnp.pad(first_pass, ((0, 0), (1, 1), (1, 1))), east_pad, north_pad)

    advected = lax.map(advect, (state, east_wind, north_wind))
    mixed = diffuse(advected, kappa)
    row_part = CX // N_GX
    col_part = CY // N_GY
    chosen = mixed[:, :PHYS_FIELDS].astype(jnp.bfloat16)
    shaped = chosen.reshape(LEVELS, PHYS_FIELDS, N_GX, row_part, N_GX, N_GY, col_part, N_GY)
    inputs = shaped.transpose(4, 7, 2, 5, 3, 6, 1, 0).reshape(N_GX * N_GY, CX * CY, FEATURES)
    cot_blocks = cotangent.reshape(N_GX * N_GY, CX * CY, FEATURES)
    tend, adjoint = lax.map(lambda pair: physics(pair[0], pair[1], w_in, w_mid, w_out), (inputs, cot_blocks))
    tend_grid = tend.reshape(N_GX, N_GY, N_GX, N_GY, row_part, col_part, PHYS_FIELDS, LEVELS)
    tend_grid = tend_grid.transpose(7, 6, 2, 4, 0, 3, 5, 1).reshape(LEVELS, PHYS_FIELDS, NX, NY)
    new_state = jnp.concatenate([mixed[:, :PHYS_FIELDS] + tend_grid.astype(jnp.float32), mixed[:, PHYS_FIELDS:]], axis=1)
    return new_state, adjoint.reshape(COLUMNS, FEATURES)
```

```python
import functools

import jax
import jax.numpy as jnp
from jax import lax
from jax.experimental import pallas as pl
from jax.experimental.pallas import tpu as pltpu
from jax.sharding import PartitionSpec as P

F32 = jnp.float32
BF16 = jnp.bfloat16
LEVELS, FIELDS, ROWS, COLS = 64, 8, 16, 128
KINDS = 4
HIDDEN, FEATURES = 512, 256
HALF = LEVELS // 2
ROW_MESSAGE = 2 * LEVELS * FIELDS + 3 * LEVELS
COL_MESSAGE = 2 * (FIELDS * ROWS + 2 * ROWS + 3 * FIELDS)
UNROLL = 4


def at_end(axis):
    return lax.axis_index(axis) == lax.axis_size(axis) - 1


def lanes(shape):
    return lax.broadcasted_iota(jnp.int32, shape, len(shape) - 1)


def rows_kernel(state, east, north, up, down):
    closed = (lanes((LEVELS, COLS)) == COLS - 1) & at_end("gy")
    count = LEVELS * FIELDS
    for out, near, far in ((up, ROWS - 1, ROWS - 2), (down, 0, 1)):
        out[0:count, :] = state[pl.ds(near, count, stride=ROWS), :].astype(BF16)
        out[count : 2 * count, :] = state[pl.ds(far, count, stride=ROWS), :].astype(BF16)
        base = 2 * count
        out[base : base + LEVELS, :] = east[pl.ds(near, LEVELS, stride=ROWS), :].astype(BF16)
        out[base + LEVELS : base + 2 * LEVELS, :] = east[pl.ds(far, LEVELS, stride=ROWS), :].astype(BF16)
        north_near = north[pl.ds(near, LEVELS, stride=ROWS), :]
        out[base + 2 * LEVELS : base + 3 * LEVELS, :] = jnp.where(closed, 0.0, north_near).astype(BF16)


def spread_winds(winds, above, below):
    base = 2 * LEVELS * FIELDS
    winds[0 : 3 * LEVELS, :] = above[base : base + 3 * LEVELS, :].astype(F32)
    winds[3 * LEVELS : 4 * LEVELS, :] = below[base : base + LEVELS, :].astype(F32)
    winds[4 * LEVELS : 5 * LEVELS, :] = below[base + 2 * LEVELS : base + 3 * LEVELS, :].astype(F32)
    winds[5 * LEVELS : 8 * LEVELS, :] = jnp.zeros((3 * LEVELS, COLS), F32)


def cols_kernel(state, east, north, above, below, out, winds, first, last):
    count = LEVELS * FIELDS
    spread_winds(winds, above, below)
    first[...] = above[0:count, :].astype(F32)
    last[...] = below[0:count, :].astype(F32)
    per_level = FIELDS * ROWS
    done = []
    for b in range(2):

        def body(i, totals):
            level = b * HALF + i
            tiles = (
                state[pl.ds(pl.multiple_of(level * per_level, per_level), per_level), :],
                east[pl.ds(pl.multiple_of(level * ROWS, ROWS), ROWS), :],
                north[pl.ds(pl.multiple_of(level * ROWS, ROWS), ROWS), :],
                first[pl.ds(pl.multiple_of(level * FIELDS, FIELDS), FIELDS), :],
                last[pl.ds(pl.multiple_of(level * FIELDS, FIELDS), FIELDS), :],
                winds[pl.ds(level, 8, stride=LEVELS), :],
            )
            merged = []
            for tile, total in zip(tiles, totals):
                mine = (lanes(tile.shape) // 4) == i
                merged.append(jnp.where(mine, pltpu.roll(tile, 2 + 4 * i, 1), total))
            return tuple(merged)

        shapes = (per_level, ROWS, ROWS, FIELDS, FIELDS, 8)
        start = tuple(jnp.zeros((n, COLS), F32) for n in shapes)
        done.append(lax.fori_loop(0, HALF, body, start, unroll=UNROLL))
    row = lax.broadcasted_iota(jnp.int32, (ROWS, COLS), 0)
    lane = lanes((ROWS, COLS))
    for b in range(2):
        fields, east_edge, north_edge = done[b][:3]
        east_edge = jnp.where((row == ROWS - 1) & at_end("gx"), 0.0, east_edge)
        north_edge = jnp.where((lane % 4 == 1) & at_end("gy"), 0.0, north_edge)
        out[b * per_level : (b + 1) * per_level, :] = fields.astype(BF16)
        base = 2 * per_level
        out[base + b * ROWS : base + (b + 1) * ROWS, :] = east_edge.astype(BF16)
        base += 2 * ROWS
        out[base + b * ROWS : base + (b + 1) * ROWS, :] = north_edge.astype(BF16)
    base = 2 * per_level + 4 * ROWS
    for n in range(3):
        both = jnp.concatenate([done[0][3 + n], done[1][3 + n]], axis=0)
        out[base + 16 * n : base + 16 * (n + 1), :] = both.astype(BF16)


def pivots_kernel(kappa, ratio, gain, inverse):
    zero = jnp.zeros((ROWS, COLS), F32)

    def body(level, carry):
        below, ratio_prev = carry
        here = pl.ds(pl.multiple_of(level * ROWS, ROWS), ROWS)
        above = jnp.where(level == LEVELS - 1, 0.0, kappa[pl.ds(pl.multiple_of(jnp.minimum(level, LEVELS - 2) * ROWS, ROWS), ROWS), :])
        flipped = 1.0 / (1.0 + below + above - below * ratio_prev)
        ratio_next = above * flipped
        ratio[here, :] = ratio_next
        gain[here, :] = below * flipped
        inverse[here, :] = flipped
        return above, ratio_next

    lax.fori_loop(0, LEVELS, body, (zero, zero), unroll=UNROLL)


def coefficients(east_up, east, north_left, north):
    zero = 0.0
    east_plus, east_minus = jnp.maximum(east_up, zero), jnp.minimum(east, zero)
    north_plus, north_minus = jnp.maximum(north_left, zero), jnp.minimum(north, zero)
    centre = (
        1.0
        - (jnp.maximum(east, zero) - jnp.minimum(east_up, zero))
        - (jnp.maximum(north, zero) - jnp.minimum(north_left, zero))
    )
    return centre, east_plus, -east_minus, north_plus, -north_minus


def combine(coefs, here, up, down, left, right):
    centre, from_up, from_down, from_left, from_right = coefs
    return centre * here + (from_up * up + from_down * down) + (from_left * left + from_right * right)


def beside(tile, edge, lane):
    axis = tile.ndim - 1
    left = pltpu.roll(jnp.where(lane == COLS - 1, edge, tile), 1, axis)
    right = pltpu.roll(jnp.where(lane == 0, edge, tile), COLS - 1, axis)
    return left, right


def advance(begin, refs, solved, scratch):
    state, east, north, above, below, own, west, far_east, ratio, gain, inverse = refs
    winds, near_up, near_down, pass_up, pass_down, edge_state, edge_pass, edge_north, edge_rows, pads = scratch
    count = LEVELS * FIELDS
    per_level = FIELDS * ROWS
    spread_winds(winds, above, below)
    near_up[...] = above[0:count, :].astype(F32)
    near_down[...] = below[0:count, :].astype(F32)
    last_row, last_col = at_end("gx"), at_end("gy")

    def packed(start, size):
        kind = lanes((size, COLS)) % 4
        mine = own[start : start + size, :].astype(F32)
        theirs = jnp.where(kind < 2, west[start : start + size, :].astype(F32), far_east[start : start + size, :].astype(F32))
        return mine, theirs

    def shifted(centre, first, last, step):
        row = lax.broadcasted_iota(jnp.int32, centre.shape, centre.ndim - 2)
        up = jnp.where(row == 0, first, pltpu.roll(centre, 1, centre.ndim - 2))
        if last is None:
            return up, None
        return up, jnp.where(row == ROWS - 1, last, pltpu.roll(centre, ROWS - 1, centre.ndim - 2))

    _, rows_first = packed(2 * per_level + 4 * ROWS, 16)
    _, rows_last = packed(2 * per_level + 4 * ROWS + 16, 16)
    _, rows_wind = packed(2 * per_level + 4 * ROWS + 32, 16)
    edge_rows[0:16, :] = rows_first
    edge_rows[16:32, :] = rows_last
    edge_rows[32:48, :] = rows_wind
    for b in range(2):
        kind = lanes((ROWS, COLS)) % 4
        _, east_edge = packed(2 * per_level + b * ROWS, ROWS)
        north_own, north_edge = packed(2 * per_level + 2 * ROWS + b * ROWS, ROWS)
        edge_north[b * ROWS : (b + 1) * ROWS, :] = north_edge
        north_left = jnp.where(kind == 1, pltpu.roll(north_edge, 1, 1), pltpu.roll(north_own, 1, 1))
        east_up, _ = shifted(east_edge, rows_wind[8 * b : 8 * b + 1, :], None, 1)
        coefs = coefficients(east_up, east_edge, north_left, north_edge)
        for f in range(begin, begin + KINDS):
            at = b * per_level + f * ROWS
            mine, here = packed(at, ROWS)
            edge_state[at : at + ROWS, :] = here
            left = jnp.where(kind == 1, pltpu.roll(here, 1, 1), pltpu.roll(mine, 1, 1))
            right = jnp.where(kind == 1, pltpu.roll(mine, COLS - 1, 1), pltpu.roll(here, COLS - 1, 1))
            n = 8 * b + f
            up, down = shifted(here, rows_first[n : n + 1, :], rows_last[n : n + 1, :], 1)
            edge_pass[at : at + ROWS, :] = combine(coefs, here, up, down, left, right)

    lane8 = lanes((8, COLS))
    lane16 = lanes((ROWS, COLS))
    lane3 = lanes((KINDS, ROWS, COLS))
    row16 = lax.broadcasted_iota(jnp.int32, (ROWS, COLS), 0)

    def one_level(level, slot, previous):
        b, i = level // HALF, level % HALF
        unpack = 4 * (HALF - 1 - i) + 2
        at8 = pl.ds(pl.multiple_of(level * FIELDS, FIELDS), FIELDS)
        wind = winds[pl.ds(level, 8, stride=LEVELS), :]
        wind_edge = pltpu.roll(edge_rows[pl.ds(pl.multiple_of(32 + 8 * b, 8), 8), :], unpack, 1)
        wind_left = pltpu.roll(jnp.where(lane8 == COLS - 1, wind_edge, wind), 1, 1)
        at16 = pl.ds(pl.multiple_of(level * ROWS, ROWS), ROWS)
        east_here = jnp.where((row16 == ROWS - 1) & last_row, 0.0, east[at16, :])
        north_here = jnp.where((lane16 == COLS - 1) & last_col, 0.0, north[at16, :])
        base = level * per_level
        up_near, up_far = near_up[at8, :], above[pl.ds(pl.multiple_of(count + 8 * level, 8), 8), :].astype(F32)
        down_near, down_far = near_down[at8, :], below[pl.ds(pl.multiple_of(count + 8 * level, 8), 8), :].astype(F32)
        row_first = state[pl.ds(base, FIELDS, stride=ROWS), :]
        row_last = state[pl.ds(base + ROWS - 1, FIELDS, stride=ROWS), :]
        edge_up = pltpu.roll(edge_rows[pl.ds(pl.multiple_of(8 * b, 8), 8), :], unpack, 1)
        left, right = beside(up_near, edge_up, lane8)
        coefs = coefficients(wind[1:2], wind[0:1], wind_left[2:3], wind[2:3])
        pass_up[slot] = combine(coefs, up_near, up_far, row_first, left, right)
        edge_down = pltpu.roll(edge_rows[pl.ds(pl.multiple_of(16 + 8 * b, 8), 8), :], unpack, 1)
        left, right = beside(down_near, edge_down, lane8)
        coefs = coefficients(east_here[ROWS - 1 : ROWS], wind[3:4], wind_left[4:5], wind[4:5])
        pass_down[slot] = combine(coefs, down_near, row_last, down_far, left, right)

        east_up = jnp.where(row16 == 0, wind[0:1], pltpu.roll(east_here, 1, 0))
        north_edge = pltpu.roll(edge_north[pl.ds(pl.multiple_of(ROWS * b, ROWS), ROWS), :], unpack, 1)
        north_left = pltpu.roll(jnp.where(lane16 == COLS - 1, north_edge, north_here), 1, 1)
        coefs = tuple(c[None] for c in coefficients(east_up, east_here, north_left, north_here))
        mine = pl.ds(pl.multiple_of(base + begin * ROWS, KINDS * ROWS), KINDS * ROWS)
        edges = pl.ds(pl.multiple_of(b * per_level + begin * ROWS, KINDS * ROWS), KINDS * ROWS)
        tile = state[mine, :].reshape(KINDS, ROWS, COLS)
        for step in range(2):
            pad = pads.at[2 * slot + step]
            pad[:, 8:24, :] = tile
            for f in range(KINDS):
                if step == 0:
                    pad[f, 7:8, :] = near_up[pl.ds(level * FIELDS + begin + f, 1), :]
                    pad[f, 24:25, :] = near_down[pl.ds(level * FIELDS + begin + f, 1), :]
                else:
                    pad[f, 7:8, :] = pass_up[slot, begin + f : begin + f + 1, :]
                    pad[f, 24:25, :] = pass_down[slot, begin + f : begin + f + 1, :]
            edge = (edge_state, edge_pass)[step][edges, :]
            edge = pltpu.roll(edge, unpack, 1).reshape(KINDS, ROWS, COLS)
            left, right = beside(tile, edge, lane3)
            tile = combine(coefs, tile, pad[:, 7:23, :], pad[:, 9:25, :], left, right)
        rhs = tile * inverse[at16, :][None] + gain[at16, :][None] * previous
        for f in range(KINDS):
            solved[pl.ds(pl.multiple_of((f * LEVELS + level) * ROWS, ROWS), ROWS), :] = rhs[f]
        return rhs

    def downward(step, previous):
        for slot in range(UNROLL):
            previous = one_level(step * UNROLL + slot, slot, previous)
        return previous

    zero = jnp.zeros((KINDS, ROWS, COLS), F32)
    lax.fori_loop(0, LEVELS // UNROLL, downward, zero)

    def upward(step, found):
        level = LEVELS - 1 - step
        factor = ratio[pl.ds(pl.multiple_of(level * ROWS, ROWS), ROWS), :]
        after = []
        for f in range(KINDS):
            here = pl.ds(pl.multiple_of((f * LEVELS + level) * ROWS, ROWS), ROWS)
            value = solved[here, :] + factor * found[f]
            solved[here, :] = value
            after.append(value)
        return tuple(after)

    lax.fori_loop(0, LEVELS, upward, tuple(jnp.zeros((ROWS, COLS), F32) for _ in range(KINDS)), unroll=UNROLL)


def advance_scratch():
    rows = LEVELS * FIELDS
    return [
        pltpu.VMEM((8 * LEVELS, COLS), F32),
        pltpu.VMEM((rows, COLS), F32),
        pltpu.VMEM((rows, COLS), F32),
        pltpu.VMEM((UNROLL, FIELDS, COLS), F32),
        pltpu.VMEM((UNROLL, FIELDS, COLS), F32),
        pltpu.VMEM((2 * FIELDS * ROWS, COLS), F32),
        pltpu.VMEM((2 * FIELDS * ROWS, COLS), F32),
        pltpu.VMEM((2 * ROWS, COLS), F32),
        pltpu.VMEM((48, COLS), F32),
        pltpu.VMEM((2 * UNROLL, KINDS, 32, COLS), F32),
    ]


def first_kernel(*refs):
    advance(0, refs[:11], refs[11], refs[12:])


def sigmoid(values):
    return 0.5 * jnp.tanh(0.5 * values) + 0.5


def dot(left, right):
    return jnp.dot(left, right, preferred_element_type=F32)


def dot_last(left, right):
    return lax.dot_general(left, right, (((1,), (1,)), ((), ())), preferred_element_type=F32)


def physics_kernel(solved, cotan, w_in_t, w_mid_t, w_out, w_mid, w_in, adjoint, active):
    row = lax.broadcasted_iota(jnp.int32, (COLS, COLS), 0)
    col = lax.broadcasted_iota(jnp.int32, (COLS, COLS), 1)
    to_slab = (row == (col % 16) * 8 + col // 16).astype(BF16)
    to_physics = (col == (row % 16) * 8 + row // 16).astype(BF16)

    def body(step, _):
        r = 2 * step
        parts = [solved[pl.ds(r + k, FEATURES, stride=ROWS), :].astype(BF16) for k in range(2)]
        inputs = jnp.concatenate(parts, axis=1)
        first = dot(w_in_t[...], inputs)
        gate = sigmoid(first)
        value = first * gate
        slope_one = gate * (1.0 + first - value)
        second = dot(w_mid_t[...], value.astype(BF16))
        gate = sigmoid(second)
        value = second * gate
        slope_two = gate * (1.0 + second - value)
        act_two = value.astype(BF16)
        active[pl.ds(pl.multiple_of(step * HIDDEN, HIDDEN), HIDDEN), :] = act_two
        blocks = [pl.ds(pl.multiple_of((r + k) * COLS, COLS), COLS) for k in range(2)]
        moved = jnp.concatenate([dot(to_slab, cotan[at, :]).astype(BF16) for at in blocks], axis=0)
        delta_two = (dot_last(w_out[...], moved) * slope_two).astype(BF16)
        delta_one = (dot(w_mid[...], delta_two) * slope_one).astype(BF16)
        back = dot(w_in[...], delta_one).astype(BF16)
        for k in range(2):
            adjoint[blocks[k], :] = dot_last(to_physics, back[:, k * COLS : (k + 1) * COLS]).astype(BF16)
        return 0

    lax.fori_loop(0, ROWS // 2, body, 0)


def last_kernel(*refs):
    ins, (solved, active, w_out_t), out, scratch = refs[:11], refs[11:14], refs[14], refs[15:]
    other = scratch[0]
    advance(KINDS, ins, other, scratch[1:])

    def body(step, _):
        tend = dot(w_out_t[...], active[pl.ds(pl.multiple_of(step * HIDDEN, HIDDEN), HIDDEN), :])
        tend = tend.astype(BF16).astype(F32)
        for k in range(2):
            r = 2 * step + k
            for f in range(KINDS):
                mixed = solved[pl.ds(f * LEVELS * ROWS + r, LEVELS, stride=ROWS), :]
                mixed = mixed + tend[f * LEVELS : (f + 1) * LEVELS, k * COLS : (k + 1) * COLS]
                out[pl.ds(f * ROWS + r, LEVELS, stride=FIELDS * ROWS), :] = mixed
        return 0

    lax.fori_loop(0, ROWS // 2, body, 0)

    def copy(level, _):
        for f in range(KINDS):
            here = pl.ds(pl.multiple_of((f * LEVELS + level) * ROWS, ROWS), ROWS)
            there = pl.ds(pl.multiple_of((level * FIELDS + KINDS + f) * ROWS, ROWS), ROWS)
            out[there, :] = other[here, :]
        return 0

    lax.fori_loop(0, LEVELS, copy, 0, unroll=UNROLL)


def run(kernel, outs, scratch, flops, moved, *args, name=None):
    return pl.pallas_call(
        kernel,
        out_shape=[jax.ShapeDtypeStruct(shape, kind) for shape, kind in outs],
        scratch_shapes=scratch,
        compiler_params=pltpu.CompilerParams(vmem_limit_bytes=48 * 1024 * 1024),
        cost_estimate=pl.CostEstimate(flops=flops, bytes_accessed=moved, transcendentals=0),
        name=name,
    )(*args)


def shift(block, axis, step):
    peers = lax.axis_size(axis)
    pairs = [(i, i + step) for i in range(peers) if 0 <= i + step < peers]
    return lax.ppermute(block, axis, pairs)


def exchange(blocks):
    return lax.all_to_all(blocks, ("gx", "gy"), split_axis=0, concat_axis=0, tiled=True)


def shards(state, east_wind, north_wind, kappa, w_in, w_mid, w_out, cotangent):
    devices = lax.axis_size("gx") * lax.axis_size("gy")
    flat = state.reshape(LEVELS * FIELDS * ROWS, COLS)
    east = east_wind.reshape(LEVELS * ROWS, COLS)
    north = north_wind.reshape(LEVELS * ROWS, COLS)
    message = ((ROW_MESSAGE, COLS), BF16)
    up, down = run(rows_kernel, [message, message], [], 10**6, 5 * 10**6, flat, east, north, name="rows")
    above = shift(up, "gx", 1)
    below = shift(down, "gx", -1)
    arrived = exchange(cotangent.reshape(devices, ROWS * COLS // devices, FEATURES))
    rows = LEVELS * FIELDS
    (own,) = run(
        cols_kernel,
        [((COL_MESSAGE, COLS), BF16)],
        [pltpu.VMEM((8 * LEVELS, COLS), F32), pltpu.VMEM((rows, COLS), F32), pltpu.VMEM((rows, COLS), F32)],
        10**6, 5 * 10**6, flat, east, north, above, below, name="cols",
    )
    west = shift(own, "gy", 1)
    far_east = shift(own, "gy", -1)
    plane = ((LEVELS * ROWS, COLS), F32)
    ratio, gain, inverse = run(
        pivots_kernel, [plane] * 3, [], 10**6, 2 * 10**6, kappa.reshape((LEVELS - 1) * ROWS, COLS), name="pivots"
    )
    ins = (flat, east, north, above, below, own, west, far_east, ratio, gain, inverse)
    slab = ((KINDS * LEVELS * ROWS, COLS), F32)
    (solved,) = run(first_kernel, [slab], advance_scratch(), 10**8, 10**7, *ins, name="first_fields")
    cotan = arrived.reshape(ROWS * COLS, FEATURES)
    adjoint, active = run(
        physics_kernel,
        [((ROWS * COLS, FEATURES), BF16), ((ROWS // 2 * HIDDEN, 2 * COLS), BF16)],
        [], 4 * 10**9, 10**7, solved, cotan, w_in.T, w_mid.T, w_out, w_mid, w_in, name="physics",
    )
    returned = exchange(adjoint.reshape(devices, ROWS * COLS // devices, FEATURES))
    scratch = [pltpu.VMEM((KINDS * LEVELS * ROWS, COLS), F32)] + advance_scratch()
    (new_state,) = run(
        last_kernel, [((LEVELS * FIELDS * ROWS, COLS), F32)], scratch, 10**9, 2 * 10**7,
        *ins, solved, active, w_out.T, name="last_fields",
    )
    return new_state.reshape(state.shape), returned.reshape(ROWS * COLS, FEATURES)


def solution(mesh):
    in_specs = (
        P(None, None, "gx", "gy"),
        P(None, "gx", "gy"),
        P(None, "gx", "gy"),
        P(None, "gx", "gy"),
        P(),
        P(),
        P(),
        P(("gx", "gy"), None),
    )
    out_specs = (P(None, None, "gx", "gy"), P(("gx", "gy"), None))
    return jax.shard_map(shards, mesh=mesh, in_specs=in_specs, out_specs=out_specs, check_vma=False)
```

```python
import functools

import jax
import jax.numpy as jnp
from jax import lax
from jax.experimental import pallas as pl
from jax.experimental.pallas import tpu as pltpu
from jax.sharding import PartitionSpec as P

F32 = jnp.float32
BF16 = jnp.bfloat16
LEVELS, FIELDS, ROWS, COLS = 64, 8, 16, 128
KINDS = 4
HIDDEN, FEATURES = 512, 256
HALF = LEVELS // 2
ROW_MESSAGE = 2 * LEVELS * FIELDS + 3 * LEVELS
COL_MESSAGE = 2 * (FIELDS * ROWS + 2 * ROWS + 3 * FIELDS)
UNROLL = 4


def at_end(axis):
    return lax.axis_index(axis) == lax.axis_size(axis) - 1


def lanes(shape):
    return lax.broadcasted_iota(jnp.int32, shape, len(shape) - 1)


def is_odd(axis):
    return lax.axis_index(axis) % 2 == 1


def rows_kernel(state, east, north, partner, other):
    closed = (lanes((LEVELS, COLS)) == COLS - 1) & at_end("gy")
    count = LEVELS * FIELDS

    def fill(out, near, far):
        for f in range(FIELDS):
            at = f * LEVELS
            out[at : at + LEVELS, :] = state[pl.ds(f * ROWS + near, LEVELS, stride=FIELDS * ROWS), :].astype(BF16)
            at += count
            out[at : at + LEVELS, :] = state[pl.ds(f * ROWS + far, LEVELS, stride=FIELDS * ROWS), :].astype(BF16)
        base = 2 * count
        out[base : base + LEVELS, :] = east[pl.ds(near, LEVELS, stride=ROWS), :].astype(BF16)
        out[base + LEVELS : base + 2 * LEVELS, :] = east[pl.ds(far, LEVELS, stride=ROWS), :].astype(BF16)
        north_near = north[pl.ds(near, LEVELS, stride=ROWS), :]
        out[base + 2 * LEVELS : base + 3 * LEVELS, :] = jnp.where(closed, 0.0, north_near).astype(BF16)

    @pl.when(is_odd("gx"))
    def _():
        fill(partner, 0, 1)
        fill(other, ROWS - 1, ROWS - 2)

    @pl.when(~is_odd("gx"))
    def _():
        fill(partner, ROWS - 1, ROWS - 2)
        fill(other, 0, 1)


def spread_winds(winds, above, below):
    base = 2 * LEVELS * FIELDS
    winds[0 : 3 * LEVELS, :] = above[base : base + 3 * LEVELS, :].astype(winds.dtype)
    winds[3 * LEVELS : 4 * LEVELS, :] = below[base : base + LEVELS, :].astype(winds.dtype)
    winds[4 * LEVELS : 5 * LEVELS, :] = below[base + 2 * LEVELS : base + 3 * LEVELS, :].astype(winds.dtype)
    winds[5 * LEVELS : 8 * LEVELS, :] = jnp.zeros((3 * LEVELS, COLS), winds.dtype)


def ones_where(shape, rule):
    row = lax.broadcasted_iota(jnp.int32, shape, 0)
    col = lax.broadcasted_iota(jnp.int32, shape, 1)
    return jnp.where(rule(row, col), 1.0, 0.0).astype(BF16)


def edge_matrix():
    return ones_where((COLS, COLS), lambda row, col: (row + 2) % COLS == col % 4)


def cols_kernel(state, east, north, w_in, w_mid, w_out, out, *prepared):
    prepare(w_in, w_mid, w_out, *prepared)
    per_level = FIELDS * ROWS
    gather = edge_matrix()
    row = lax.broadcasted_iota(jnp.int32, (ROWS, COLS), 0)
    lane = lanes((ROWS, COLS))
    many = 16
    for b in range(2):

        def body(step, totals):
            level = b * HALF + step * many
            merged = list(totals)
            for n, (ref, size) in enumerate(((state, per_level), (east, ROWS), (north, ROWS))):
                at = pl.ds(pl.multiple_of(level * size, size), many * size)
                edges = dot(ref[at, :].astype(BF16), gather)
                for k in range(many):
                    mine = (lanes((size, COLS)) // 4) == step * many + k
                    merged[n] = jnp.where(mine, edges[k * size : (k + 1) * size], merged[n])
            return tuple(merged)

        start = tuple(jnp.zeros((n, COLS), F32) for n in (per_level, ROWS, ROWS))
        fields, east_edge, north_edge = lax.fori_loop(0, HALF // many, body, start)
        east_edge = jnp.where((row == ROWS - 1) & at_end("gx"), 0.0, east_edge)
        north_edge = jnp.where((lane % 4 == 1) & at_end("gy"), 0.0, north_edge)
        out[b * per_level : (b + 1) * per_level, :] = fields.astype(BF16)
        base = 2 * per_level
        out[base + b * ROWS : base + (b + 1) * ROWS, :] = east_edge.astype(BF16)
        base += 2 * ROWS
        out[base + b * ROWS : base + (b + 1) * ROWS, :] = north_edge.astype(BF16)


def corners_kernel(edges, from_partner, from_other, out, winds):
    @pl.when(is_odd("gx"))
    def _():
        corners(edges, from_partner, from_other, out, winds)

    @pl.when(~is_odd("gx"))
    def _():
        corners(edges, from_other, from_partner, out, winds)


def corners(edges, above, below, out, winds):
    count = LEVELS * FIELDS
    spread_winds(winds, above, below)
    gather = edge_matrix()
    collect = ones_where(
        (16, count), lambda row, col: (row % 8 == col // LEVELS) & (row // 8 == (col % LEVELS) // HALF)
    )
    level = lax.broadcasted_iota(jnp.int32, (count, COLS), 0) % HALF
    mine = lanes((count, COLS)) // 4 == level
    size = edges.shape[0]
    out[0:size, :] = edges[...]
    for n, source in enumerate((above[0:count, :], below[0:count, :], winds[...])):
        spread = jnp.where(mine, dot(source, gather), 0.0).astype(BF16)
        out[size + 16 * n : size + 16 * (n + 1), :] = dot(collect, spread).astype(BF16)


def prepare(w_in, w_mid, w_out, w_in_t, w_mid_t, w_out_t):
    by_level = ones_where(
        (FEATURES, FEATURES), lambda row, col: row == (col % KINDS) * LEVELS + col // KINDS
    )
    w_in_t[...] = dot(w_in[...].T, by_level).astype(BF16)
    w_mid_t[...] = w_mid[...].T
    w_out_t[...] = dot(w_out[...], by_level).astype(BF16).T


def coefficients(east_up, east, north_left, north):
    zero = 0.0
    east_plus, east_minus = jnp.maximum(east_up, zero), jnp.minimum(east, zero)
    north_plus, north_minus = jnp.maximum(north_left, zero), jnp.minimum(north, zero)
    centre = (
        1.0
        - (jnp.maximum(east, zero) - jnp.minimum(east_up, zero))
        - (jnp.maximum(north, zero) - jnp.minimum(north_left, zero))
    )
    return centre, east_plus, -east_minus, north_plus, -north_minus


def combine(coefs, here, up, down, left, right):
    centre, from_up, from_down, from_left, from_right = coefs
    return centre * here + (from_up * up + from_down * down) + (from_left * left + from_right * right)


def beside_matrix():
    def rule(row, col):
        lane, place = row % COLS, col % COLS
        inside = either(col < COLS, lane + 1 == place, lane == place + 1)
        halo = either(col < COLS, (place == 0) & (lane % 4 == 1), (place == COLS - 1) & (lane % 4 == 2))
        return either(row < 2 * COLS, inside, halo)

    return ones_where((3 * COLS, 2 * COLS), rule)


def strip_matrix():
    def rule(row, col):
        lane, place = row % COLS, col % COLS
        theirs = row < COLS
        one, two = place % 4 == 1, place % 4 == 2
        left = (lane + 1 == place) & either(theirs, one, two)
        right = (lane == place + 1) & either(theirs, two, one)
        return either(col < COLS, left, right)

    return ones_where((2 * COLS, 2 * COLS), rule)


def either(choice, yes, no):
    return (choice & yes) | (~choice & no)


def high_low(values):
    high = values.astype(BF16)
    return high, (values - high.astype(F32)).astype(BF16)


BATCH = 32
SLICE = KINDS * ROWS


def advance(begin, refs, each_start, each_batch, scratch):
    state, far_east_wind, far_north, far_kappa, rows_partner, rows_other, own, from_partner, from_other = refs
    (above, below, held, winds, near_up, near_down, pass_up, pass_down, edge_state, edge_pass, edge_north, first_pass,
     moving, moving_north, beside_map, east, north, kappa, ratio, sems) = scratch
    count = LEVELS * FIELDS
    per_level = FIELDS * ROWS
    batches = LEVELS // BATCH
    copies = [
        pltpu.make_async_copy(
            state.at[pl.ds(n * BATCH, BATCH), pl.ds(begin * ROWS, SLICE), :],
            held.at[pl.ds(1 + n * BATCH, BATCH)],
            sems.at[n],
        )
        for n in range(batches)
    ]
    planes = ((far_east_wind, east), (far_north, north), (far_kappa, kappa))
    later = [pltpu.make_async_copy(there, here, sems.at[batches + n]) for n, (there, here) in enumerate(planes)]
    for copy in [later[0]] + copies + later[1:]:
        copy.start()
    each_start()

    @pl.when(is_odd("gx"))
    def _():
        above[...] = rows_partner[...]
        below[...] = rows_other[...]

    @pl.when(~is_odd("gx"))
    def _():
        above[...] = rows_other[...]
        below[...] = rows_partner[...]

    beside_map[...] = beside_matrix()
    spread_winds(winds, above, below)
    kinds = KINDS * LEVELS
    near_up[0:kinds, :] = above[begin * LEVELS : begin * LEVELS + kinds, :].astype(F32)
    near_up[kinds : kinds + 8, :] = jnp.zeros((8, COLS), F32)
    near_down[0:8, :] = jnp.zeros((8, COLS), F32)
    near_down[8 : kinds + 8, :] = below[begin * LEVELS : begin * LEVELS + kinds, :].astype(F32)
    pass_up[kinds : kinds + 8, :] = jnp.zeros((8, COLS), F32)
    pass_down[0:8, :] = jnp.zeros((8, COLS), F32)
    last_row, last_col = at_end("gx"), at_end("gy")
    row16 = lax.broadcasted_iota(jnp.int32, (ROWS, COLS), 0)
    lane16 = lanes((ROWS, COLS))
    row8 = lax.broadcasted_iota(jnp.int32, (8, COLS), 0)
    group = lanes((ROWS, COLS)) // 4

    def packed(start, size):
        kind = lanes((size, COLS)) % 4
        partner, other = from_partner[start : start + size, :].astype(F32), from_other[start : start + size, :].astype(F32)
        theirs = jnp.where((kind < 2) == is_odd("gy"), partner, other)
        return own[start : start + size, :], theirs

    def shifted(centre, first, last):
        up = jnp.where(row16 == 0, first, pltpu.roll(centre, 1, 0))
        if last is None:
            return up, None
        return up, jnp.where(row16 == ROWS - 1, last, pltpu.roll(centre, ROWS - 1, 0))

    _, rows_first = packed(2 * per_level + 4 * ROWS, 16)
    _, rows_last = packed(2 * per_level + 4 * ROWS + 16, 16)
    _, rows_wind = packed(2 * per_level + 4 * ROWS + 32, 16)
    strip_map = strip_matrix()
    _, east_edges = packed(2 * per_level, 2 * ROWS)
    own_north, north_edges = packed(2 * per_level + 2 * ROWS, 2 * ROWS)
    edge_north[...] = north_edges
    norths = dot(jnp.concatenate([north_edges.astype(BF16), own_north], axis=1), strip_map)
    for b in range(2):
        here = slice(b * ROWS, (b + 1) * ROWS)
        east_up, _ = shifted(east_edges[here], rows_wind[8 * b : 8 * b + 1, :], None)
        coefs = coefficients(east_up, east_edges[here], norths[here, :COLS], north_edges[here])
        mine, theirs = packed(b * per_level + begin * ROWS, SLICE)
        sides = dot(jnp.concatenate([theirs.astype(BF16), mine], axis=1), strip_map)
        for f in range(KINDS):
            part = slice(f * ROWS, (f + 1) * ROWS)
            n = 8 * b + begin + f
            up, down = shifted(theirs[part], rows_first[n : n + 1, :], rows_last[n : n + 1, :])
            at = b * SLICE + f * ROWS
            edge_state[at : at + ROWS, :] = theirs[part]
            edge_pass[at : at + ROWS, :] = combine(coefs, theirs[part], up, down, sides[part, :COLS], sides[part, COLS:])

    later[0].wait()
    for copy in copies:
        copy.wait()
    flat = held.reshape((LEVELS + 2) * SLICE, COLS)

    place = lax.broadcasted_iota(jnp.int32, (LEVELS, COLS), 0)
    at_level = lanes((LEVELS, COLS)) // 4 == place % HALF
    upper = place < HALF

    def spread(rows, n):
        value = jnp.where(upper, rows[n : n + 1, :], rows[8 + n : 9 + n, :])
        return jnp.where(at_level, value, 0.0).astype(BF16)

    def sides_of(values, halo):
        both = jnp.concatenate([values, halo], axis=1)
        return dot(both, beside_map[COLS : 3 * COLS, :])

    def wind_of(kind):
        return winds[kind * LEVELS : (kind + 1) * LEVELS, :]

    def strip(near, far, inner, out, offset, east_before, east_after, north_kind, corner, outward):
        north_here = wind_of(north_kind)
        north_left = sides_of(north_here.astype(BF16), spread(rows_wind, north_kind))[:, :COLS]
        coefs = coefficients(east_before, east_after, north_left, north_here)
        for f in range(KINDS):
            values = near[(begin + f) * LEVELS : (begin + f + 1) * LEVELS, :]
            sides = sides_of(values, spread(corner, begin + f))
            beyond = far[count + (begin + f) * LEVELS : count + (begin + f + 1) * LEVELS, :].astype(F32)
            within = flat[pl.ds(SLICE + f * ROWS + inner, LEVELS, stride=SLICE), :]
            up, down = (beyond, within) if outward else (within, beyond)
            at = offset + f * LEVELS
            out[at : at + LEVELS, :] = combine(coefs, values.astype(F32), up, down, sides[:, :COLS], sides[:, COLS:])

    strip(above, above, 0, pass_up, 0, wind_of(1), wind_of(0), 2, rows_first, True)
    own_last = jnp.where(last_row, 0.0, east[pl.ds(ROWS - 1, LEVELS, stride=ROWS), :])
    strip(below, below, ROWS - 1, pass_down, 8, own_last, wind_of(3), 4, rows_last, False)

    for copy in later[1:]:
        copy.wait()

    def load(moving, at, values, edge, number):
        size = values.shape[0]
        high, low = high_low(values)
        moving[at : at + size, 0:COLS] = high
        moving[at : at + size, COLS : 2 * COLS] = low
        mine = lanes((size, COLS)) // 4 == number
        moving[at : at + size, 2 * COLS : 3 * COLS] = jnp.where(mine, edge, 0.0).astype(BF16)

    def one_batch(step, carried):
        previous, coupling, factor = carried
        b = step // (batches // 2)
        edge_at = pl.ds(pl.multiple_of(b * SLICE, SLICE), SLICE)
        north_at = pl.ds(pl.multiple_of(b * ROWS, ROWS), ROWS)
        first_number = (step % (batches // 2)) * BATCH
        norths = []
        for j in range(BATCH):
            level = step * BATCH + j
            here = flat[pl.ds(pl.multiple_of((level + 1) * SLICE, SLICE), SLICE), :]
            load(moving, j * SLICE, here, edge_state[edge_at, :], first_number + j)
            north_here = north[pl.ds(pl.multiple_of(level * ROWS, ROWS), ROWS), :]
            north_here = jnp.where((lane16 == COLS - 1) & last_col, 0.0, north_here)
            norths.append(north_here)
            load(moving_north, j * ROWS, north_here, edge_north[north_at, :], first_number + j)
        north_left = dot(moving_north[...], beside_map[:, 0:COLS])
        sides = dot(moving[...], beside_map[...])
        coefs = []
        for j in range(BATCH):
            level = step * BATCH + j
            at16 = pl.ds(pl.multiple_of(level * ROWS, ROWS), ROWS)
            east_here = jnp.where((row16 == ROWS - 1) & last_row, 0.0, east[at16, :])
            east_up = jnp.where(row16 == 0, winds[pl.ds(level, 1), :], pltpu.roll(east_here, 1, 0))
            coefs.append(coefficients(east_up, east_here, north_left[j * ROWS : (j + 1) * ROWS], norths[j]))

        def stencil(source, offset, j, level, first, last):
            found = []
            for f in range(KINDS):
                at = offset + f * ROWS
                line = f * LEVELS + level
                place = j * SLICE + f * ROWS
                for half in range(2):
                    r = at + 8 * half
                    here = source[pl.ds(pl.multiple_of(r, 8), 8), :]
                    up = source[pl.ds(r - 1, 8), :]
                    down = source[pl.ds(r + 1, 8), :]
                    if half == 0:
                        up = jnp.where(row8 == 0, first[pl.ds(line, 8), :], up)
                    else:
                        down = jnp.where(row8 == 7, last[pl.ds(line + 1, 8), :], down)
                    part = slice(place + 8 * half, place + 8 * half + 8)
                    mine = tuple(c[8 * half : 8 * half + 8] for c in coefs[j])
                    found.append(combine(mine, here, up, down, sides[part, :COLS], sides[part, COLS:]))
            return jnp.concatenate(found, axis=0)

        for j in range(BATCH):
            level = step * BATCH + j
            value = stencil(flat, (level + 1) * SLICE, j, level, near_up, near_down)
            first_pass[8 + j * SLICE : 8 + (j + 1) * SLICE, :] = value
            load(moving, j * SLICE, value, edge_pass[edge_at, :], first_number + j)
        sides = dot(moving[...], beside_map[...])
        for j in range(BATCH):
            level = step * BATCH + j
            value = stencil(first_pass, 8 + j * SLICE, j, level, pass_up, pass_down)
            at16 = pl.ds(pl.multiple_of(level * ROWS, ROWS), ROWS)
            next_at = pl.ds(pl.multiple_of(jnp.minimum(level, LEVELS - 2) * ROWS, ROWS), ROWS)
            next_coupling = jnp.where(level == LEVELS - 1, 0.0, kappa[next_at, :])
            flipped = 1.0 / (1.0 + coupling + next_coupling - coupling * factor)
            keep = coupling * flipped
            factor = next_coupling * flipped
            ratio[at16, :] = factor
            coupling = next_coupling
            after = []
            for f in range(KINDS):
                rhs = value[f * ROWS : (f + 1) * ROWS] * flipped + keep * previous[f]
                flat[pl.ds(pl.multiple_of((level + 1) * SLICE + f * ROWS, ROWS), ROWS), :] = rhs
                after.append(rhs)
            previous = tuple(after)
        return previous, coupling, factor

    start = tuple(jnp.zeros((ROWS, COLS), F32) for _ in range(KINDS))
    first_pass[0:8, :] = jnp.zeros((8, COLS), F32)
    first_pass[8 + BATCH * SLICE : 16 + BATCH * SLICE, :] = jnp.zeros((8, COLS), F32)
    zero = jnp.zeros((ROWS, COLS), F32)
    lax.fori_loop(0, batches, one_batch, (start, zero, zero))

    found = start
    for n in reversed(range(batches)):

        def upward(step, found):
            level = (n + 1) * BATCH - 1 - step
            factor = ratio[pl.ds(pl.multiple_of(level * ROWS, ROWS), ROWS), :]
            after = []
            for f in range(KINDS):
                here = pl.ds(pl.multiple_of((level + 1) * SLICE + f * ROWS, ROWS), ROWS)
                value = flat[here, :] + factor * found[f]
                flat[here, :] = value
                after.append(value)
            return tuple(after)

        found = lax.fori_loop(0, BATCH, upward, found, unroll=UNROLL)
        each_batch(n)


def advance_scratch():
    rows = LEVELS * KINDS + 8
    return [
        pltpu.VMEM((ROW_MESSAGE, COLS), BF16),
        pltpu.VMEM((ROW_MESSAGE, COLS), BF16),
        pltpu.VMEM((LEVELS + 2, SLICE, COLS), F32),
        pltpu.VMEM((8 * LEVELS, COLS), F32),
        pltpu.VMEM((rows, COLS), F32),
        pltpu.VMEM((rows, COLS), F32),
        pltpu.VMEM((rows, COLS), F32),
        pltpu.VMEM((rows, COLS), F32),
        pltpu.VMEM((2 * SLICE, COLS), F32),
        pltpu.VMEM((2 * SLICE, COLS), F32),
        pltpu.VMEM((2 * ROWS, COLS), F32),
        pltpu.VMEM((16 + BATCH * SLICE, COLS), F32),
        pltpu.VMEM((BATCH * SLICE, 3 * COLS), BF16),
        pltpu.VMEM((BATCH * ROWS, 3 * COLS), BF16),
        pltpu.VMEM((3 * COLS, 2 * COLS), BF16),
        pltpu.VMEM((LEVELS * ROWS, COLS), F32),
        pltpu.VMEM((LEVELS * ROWS, COLS), F32),
        pltpu.VMEM(((LEVELS - 1) * ROWS, COLS), F32),
        pltpu.VMEM((LEVELS * ROWS, COLS), F32),
        pltpu.SemaphoreType.DMA((LEVELS // BATCH + 3,)),
    ]


def sigmoid(values):
    return 0.5 * jnp.tanh(0.5 * values) + 0.5


def dot(left, right):
    return jnp.dot(left, right, preferred_element_type=F32)


def dot_last(left, right):
    return lax.dot_general(left, right, (((1,), (1,)), ((), ())), preferred_element_type=F32)


GROUP = 8


def main_kernel(*refs):
    ins, far, (solved, far_adjoint, far_active) = refs[:9], refs[9:15], refs[15:18]
    near, (adjoint, active, sems), scratch = refs[18:24], refs[24:27], refs[27:]
    held = scratch[2]
    fetches = [pltpu.make_async_copy(there, here, sems.at[n]) for n, (there, here) in enumerate(zip(far, near))]
    cotan, w_in_t, w_mid_t, w_out, w_mid, w_in = near
    copies = [
        pltpu.make_async_copy(
            held.at[pl.ds(1 + n * BATCH, BATCH)], solved.at[pl.ds(n * BATCH, BATCH)], sems.at[6 + n]
        )
        for n in range(LEVELS // BATCH)
    ]

    def begin():
        for fetch in fetches:
            fetch.start()

    advance(0, ins, begin, lambda n: copies[n].start(), scratch)
    for fetch in fetches:
        fetch.wait()
    lines = held.reshape((LEVELS + 2) * SLICE, COLS)
    to_slab = ones_where((COLS, COLS), lambda row, col: row == (col % 16) * 8 + col // 16)
    to_physics = ones_where((COLS, COLS), lambda row, col: col == (row % 16) * 8 + row // 16)
    sends = []
    for step in range(ROWS // GROUP):
        rows = [GROUP * step + k for k in range(GROUP)]
        parts = [lines[pl.ds(SLICE + r, FEATURES, stride=ROWS), :].astype(BF16) for r in rows]
        inputs = jnp.concatenate(parts, axis=1)
        first = dot(w_in_t[...], inputs)
        gate = sigmoid(first)
        value = first * gate
        slope_one = gate * (1.0 + first - value)
        second = dot(w_mid_t[...], value.astype(BF16))
        gate = sigmoid(second)
        value = second * gate
        slope_two = gate * (1.0 + second - value)
        here = pl.ds(step * HIDDEN, HIDDEN)
        active[here, :] = value.astype(BF16)
        sends.append(pltpu.make_async_copy(active.at[here], far_active.at[here], sems.at[10 + 2 * step]))
        sends[-1].start()
        blocks = [slice(r * COLS, (r + 1) * COLS) for r in rows]
        moved = jnp.concatenate([dot(to_slab, cotan[at, :]).astype(BF16) for at in blocks], axis=0)
        delta_two = (dot_last(w_out[...], moved) * slope_two).astype(BF16)
        delta_one = (dot(w_mid[...], delta_two) * slope_one).astype(BF16)
        back = dot(w_in[...], delta_one).astype(BF16)
        for k, at in enumerate(blocks):
            adjoint[at, :] = dot_last(to_physics, back[:, k * COLS : (k + 1) * COLS]).astype(BF16)
        here = pl.ds(step * GROUP * COLS, GROUP * COLS)
        sends.append(pltpu.make_async_copy(adjoint.at[here], far_adjoint.at[here], sems.at[11 + 2 * step]))
        sends[-1].start()
    for copy in copies + sends:
        copy.wait()


def last_kernel(*refs):
    ins, (solved, active, w_out_t), out, (mixed, sems), scratch = refs[:9], refs[9:12], refs[12], refs[13:15], refs[15:]
    held = scratch[2]
    batches = LEVELS // BATCH
    fetch = pltpu.make_async_copy(solved, mixed, sems.at[batches + 1])
    fetch.start()
    lines = mixed.reshape(LEVELS * SLICE, COLS)
    for step in range(ROWS // GROUP):
        tend = dot(w_out_t[...], active[step * HIDDEN : (step + 1) * HIDDEN, :])
        tend = tend.astype(BF16).astype(F32)
        if step == 0:
            fetch.wait()
        for k in range(GROUP):
            here = pl.ds(GROUP * step + k, FEATURES, stride=ROWS)
            lines[here, :] = lines[here, :] + tend[:, k * COLS : (k + 1) * COLS]
    first = pltpu.make_async_copy(mixed, out.at[:, pl.ds(0, SLICE), :], sems.at[batches])
    first.start()
    copies = [
        pltpu.make_async_copy(
            held.at[pl.ds(1 + n * BATCH, BATCH)],
            out.at[pl.ds(n * BATCH, BATCH), pl.ds(SLICE, SLICE), :],
            sems.at[n],
        )
        for n in range(batches)
    ]
    advance(KINDS, ins, lambda: None, lambda n: copies[n].start(), scratch)
    first.wait()
    for copy in copies:
        copy.wait()


def run(kernel, outs, scratch, flops, moved, *args, name=None, far=(), limit=62914560, **rest):
    anywhere, near = pl.BlockSpec(memory_space=pl.ANY), pl.BlockSpec(memory_space=pltpu.VMEM)
    rest = rest or dict(in_specs=[anywhere if n in far else near for n in range(len(args))])
    return pl.pallas_call(
        kernel,
        out_shape=[jax.ShapeDtypeStruct(shape, kind) for shape, kind in outs],
        scratch_shapes=scratch,
        compiler_params=pltpu.CompilerParams(vmem_limit_bytes=limit),
        cost_estimate=pl.CostEstimate(flops=flops, bytes_accessed=moved, transcendentals=0),
        name=name,
        **rest,
    )(*args)


FAR = (0, 1, 2, 3)


def main(ins, cotan, *weights):
    near = pl.BlockSpec(memory_space=pltpu.VMEM)
    far = pl.BlockSpec(memory_space=pl.ANY)
    outs = [
        ((LEVELS, SLICE, COLS), F32),
        ((ROWS * COLS, FEATURES), BF16),
        ((ROWS // GROUP * HIDDEN, GROUP * COLS), BF16),
    ]
    held = [pltpu.VMEM(x.shape, BF16) for x in (cotan,) + weights]
    held += [pltpu.VMEM(*outs[1]), pltpu.VMEM(*outs[2]), pltpu.SemaphoreType.DMA((10 + 2 * ROWS // GROUP,))]
    return run(
        main_kernel, outs, held + advance_scratch(), 4 * 10**9, 10**7, *ins, cotan, *weights, name="main",
        in_specs=[far if n in FAR or n >= 9 else near for n in range(15)], out_specs=[far] * 3,
    )


def last(ins, solved, active, w_out_t):
    near = pl.BlockSpec(memory_space=pltpu.VMEM)
    far = pl.BlockSpec(memory_space=pl.ANY)
    mixed = [pltpu.VMEM((LEVELS, SLICE, COLS), F32), pltpu.SemaphoreType.DMA((LEVELS // BATCH + 2,))]
    (new_state,) = run(
        last_kernel, [((LEVELS, FIELDS * ROWS, COLS), F32)], mixed + advance_scratch(), 10**9, 2 * 10**7,
        *ins, solved, active, w_out_t, name="last_fields",
        in_specs=[far if n in FAR + (9,) else near for n in range(12)], out_specs=[far],
    )
    return new_state


def swap(block, axis, start):
    firsts = range(start, lax.axis_size(axis) - 1, 2)
    return lax.ppermute(block, axis, [(i, i + 1) for i in firsts] + [(i + 1, i) for i in firsts])


def exchange(blocks):
    return lax.all_to_all(blocks, ("gx", "gy"), split_axis=0, concat_axis=0, tiled=True)


def shards(state, east_wind, north_wind, kappa, w_in, w_mid, w_out, cotangent):
    devices = lax.axis_size("gx") * lax.axis_size("gy")
    flat = state.reshape(LEVELS * FIELDS * ROWS, COLS)
    east = east_wind.reshape(LEVELS * ROWS, COLS)
    north = north_wind.reshape(LEVELS * ROWS, COLS)
    message = ((ROW_MESSAGE, COLS), BF16)
    to_partner, to_other = run(rows_kernel, [message, message], [], 10**6, 5 * 10**6, flat, east, north, name="rows")
    arrived = exchange(cotangent.reshape(devices, ROWS * COLS // devices, FEATURES))
    from_other = swap(to_other, "gx", 1)
    from_partner = swap(to_partner, "gx", 0)
    count = LEVELS * FIELDS
    flipped = [(w.shape[::-1], BF16) for w in (w_in, w_mid, w_out)]
    edges, w_in_t, w_mid_t, w_out_t = run(
        cols_kernel, [((COL_MESSAGE - 48, COLS), BF16)] + flipped, [], 10**8, 10**7,
        flat, east, north, w_in, w_mid, w_out, name="cols",
    )
    (own,) = run(
        corners_kernel, [((COL_MESSAGE, COLS), BF16)], [pltpu.VMEM((count, COLS), BF16)], 10**6, 10**6,
        edges, from_partner, from_other, name="corners", limit=8 * 1024 * 1024,
    )
    rows_partner, rows_other = from_partner, from_other
    from_other = swap(own, "gy", 1)
    from_partner = swap(own, "gy", 0)
    ins = (state.reshape(LEVELS, FIELDS * ROWS, COLS), east, north, kappa.reshape((LEVELS - 1) * ROWS, COLS))
    ins += (rows_partner, rows_other, own, from_partner, from_other)
    cotan = arrived.reshape(ROWS * COLS, FEATURES)
    solved, adjoint, active = main(ins, cotan, w_in_t, w_mid_t, w_out, w_mid, w_in)
    returned = exchange(adjoint.reshape(devices, ROWS * COLS // devices, FEATURES))
    new_state = last(ins, solved, active, w_out_t)
    return new_state.reshape(state.shape), returned.reshape(ROWS * COLS, FEATURES)


def solution(mesh):
    in_specs = (
        P(None, None, "gx", "gy"),
        P(None, "gx", "gy"),
        P(None, "gx", "gy"),
        P(None, "gx", "gy"),
        P(),
        P(),
        P(),
        P(("gx", "gy"), None),
    )
    out_specs = (P(None, None, "gx", "gy"), P(("gx", "gy"), None))
    return jax.shard_map(shards, mesh=mesh, in_specs=in_specs, out_specs=out_specs, check_vma=False)
```

```python
import functools

import jax
import jax.numpy as jnp
from jax import lax
from jax.experimental import pallas as pl
from jax.experimental.pallas import tpu as pltpu
from jax.sharding import PartitionSpec as P

F32 = jnp.float32
BF16 = jnp.bfloat16
LEVELS, FIELDS, ROWS, COLS = 64, 8, 16, 128
KINDS = 4
HIDDEN, FEATURES = 512, 256
HALF = LEVELS // 2
ROW_MESSAGE = 2 * LEVELS * FIELDS + 3 * LEVELS
COL_MESSAGE = 2 * (FIELDS * ROWS + 2 * ROWS + 3 * FIELDS)
UNROLL = 4


def at_end(axis):
    return lax.axis_index(axis) == lax.axis_size(axis) - 1


def lanes(shape):
    return lax.broadcasted_iota(jnp.int32, shape, len(shape) - 1)


def is_odd(axis):
    return lax.axis_index(axis) % 2 == 1


def rows_kernel(state, east, north, partner, other):
    closed = (lanes((LEVELS, COLS)) == COLS - 1) & at_end("gy")
    count = LEVELS * FIELDS

    def fill(out, near, far):
        for f in range(FIELDS):
            at = f * LEVELS
            out[at : at + LEVELS, :] = state[pl.ds(f * ROWS + near, LEVELS, stride=FIELDS * ROWS), :].astype(BF16)
            at += count
            out[at : at + LEVELS, :] = state[pl.ds(f * ROWS + far, LEVELS, stride=FIELDS * ROWS), :].astype(BF16)
        base = 2 * count
        out[base : base + LEVELS, :] = east[pl.ds(near, LEVELS, stride=ROWS), :].astype(BF16)
        out[base + LEVELS : base + 2 * LEVELS, :] = east[pl.ds(far, LEVELS, stride=ROWS), :].astype(BF16)
        north_near = north[pl.ds(near, LEVELS, stride=ROWS), :]
        out[base + 2 * LEVELS : base + 3 * LEVELS, :] = jnp.where(closed, 0.0, north_near).astype(BF16)

    @pl.when(is_odd("gx"))
    def _():
        fill(partner, 0, 1)
        fill(other, ROWS - 1, ROWS - 2)

    @pl.when(~is_odd("gx"))
    def _():
        fill(partner, ROWS - 1, ROWS - 2)
        fill(other, 0, 1)


def spread_winds(winds, above, below):
    base = 2 * LEVELS * FIELDS
    winds[0 : 3 * LEVELS, :] = above[base : base + 3 * LEVELS, :].astype(winds.dtype)
    winds[3 * LEVELS : 4 * LEVELS, :] = below[base : base + LEVELS, :].astype(winds.dtype)
    winds[4 * LEVELS : 5 * LEVELS, :] = below[base + 2 * LEVELS : base + 3 * LEVELS, :].astype(winds.dtype)
    winds[5 * LEVELS : 8 * LEVELS, :] = jnp.zeros((3 * LEVELS, COLS), winds.dtype)


def ones_where(shape, rule):
    row = lax.broadcasted_iota(jnp.int32, shape, 0)
    col = lax.broadcasted_iota(jnp.int32, shape, 1)
    return jnp.where(rule(row, col), 1.0, 0.0).astype(BF16)


def edge_matrix():
    return ones_where((COLS, COLS), lambda row, col: (row + 2) % COLS == col % 4)


def cols_kernel(state, east, north, w_in, w_mid, w_out, out, *prepared):
    prepare(w_in, w_mid, w_out, *prepared)
    per_level = FIELDS * ROWS
    gather = edge_matrix()
    row = lax.broadcasted_iota(jnp.int32, (ROWS, COLS), 0)
    lane = lanes((ROWS, COLS))
    many = 16
    for b in range(2):

        def body(step, totals):
            level = b * HALF + step * many
            merged = list(totals)
            for n, (ref, size) in enumerate(((state, per_level), (east, ROWS), (north, ROWS))):
                at = pl.ds(pl.multiple_of(level * size, size), many * size)
                edges = dot(ref[at, :].astype(BF16), gather)
                for k in range(many):
                    mine = (lanes((size, COLS)) // 4) == step * many + k
                    merged[n] = jnp.where(mine, edges[k * size : (k + 1) * size], merged[n])
            return tuple(merged)

        start = tuple(jnp.zeros((n, COLS), F32) for n in (per_level, ROWS, ROWS))
        fields, east_edge, north_edge = lax.fori_loop(0, HALF // many, body, start)
        east_edge = jnp.where((row == ROWS - 1) & at_end("gx"), 0.0, east_edge)
        north_edge = jnp.where((lane % 4 == 1) & at_end("gy"), 0.0, north_edge)
        out[b * per_level : (b + 1) * per_level, :] = fields.astype(BF16)
        base = 2 * per_level
        out[base + b * ROWS : base + (b + 1) * ROWS, :] = east_edge.astype(BF16)
        base += 2 * ROWS
        out[base + b * ROWS : base + (b + 1) * ROWS, :] = north_edge.astype(BF16)


def corners_kernel(edges, from_partner, from_other, out, winds):
    @pl.when(is_odd("gx"))
    def _():
        corners(edges, from_partner, from_other, out, winds)

    @pl.when(~is_odd("gx"))
    def _():
        corners(edges, from_other, from_partner, out, winds)


def corners(edges, above, below, out, winds):
    count = LEVELS * FIELDS
    spread_winds(winds, above, below)
    gather = edge_matrix()
    collect = ones_where(
        (16, count), lambda row, col: (row % 8 == col // LEVELS) & (row // 8 == (col % LEVELS) // HALF)
    )
    level = lax.broadcasted_iota(jnp.int32, (count, COLS), 0) % HALF
    mine = lanes((count, COLS)) // 4 == level
    size = edges.shape[0]
    out[0:size, :] = edges[...]
    for n, source in enumerate((above[0:count, :], below[0:count, :], winds[...])):
        spread = jnp.where(mine, dot(source, gather), 0.0).astype(BF16)
        out[size + 16 * n : size + 16 * (n + 1), :] = dot(collect, spread).astype(BF16)


def prepare(w_in, w_mid, w_out, w_in_t, w_mid_t, w_out_t):
    by_level = ones_where(
        (FEATURES, FEATURES), lambda row, col: row == (col % KINDS) * LEVELS + col // KINDS
    )
    w_in_t[...] = dot(w_in[...].T, by_level).astype(BF16)
    w_mid_t[...] = w_mid[...].T
    w_out_t[...] = dot(w_out[...], by_level).astype(BF16).T


def coefficients(east_up, east, north_left, north):
    zero = 0.0
    east_plus, east_minus = jnp.maximum(east_up, zero), jnp.minimum(east, zero)
    north_plus, north_minus = jnp.maximum(north_left, zero), jnp.minimum(north, zero)
    centre = (
        1.0
        - (jnp.maximum(east, zero) - jnp.minimum(east_up, zero))
        - (jnp.maximum(north, zero) - jnp.minimum(north_left, zero))
    )
    return centre, east_plus, -east_minus, north_plus, -north_minus


def combine(coefs, here, up, down, left, right):
    centre, from_up, from_down, from_left, from_right = coefs
    return centre * here + (from_up * up + from_down * down) + (from_left * left + from_right * right)


def beside_matrix():
    def rule(row, col):
        lane, place = row % COLS, col % COLS
        inside = either(col < COLS, lane + 1 == place, lane == place + 1)
        halo = either(col < COLS, (place == 0) & (lane % 4 == 1), (place == COLS - 1) & (lane % 4 == 2))
        return either(row < COLS, inside, halo)

    return ones_where((2 * COLS, 2 * COLS), rule)


def strip_matrix():
    def rule(row, col):
        lane, place = row % COLS, col % COLS
        theirs = row < COLS
        one, two = place % 4 == 1, place % 4 == 2
        left = (lane + 1 == place) & either(theirs, one, two)
        right = (lane == place + 1) & either(theirs, two, one)
        return either(col < COLS, left, right)

    return ones_where((2 * COLS, 2 * COLS), rule)


def either(choice, yes, no):
    return (choice & yes) | (~choice & no)


BATCH = 32
SLICE = KINDS * ROWS


def advance(begin, refs, each_start, each_batch, scratch):
    state, far_east_wind, far_north, far_kappa, rows_partner, rows_other, own, from_partner, from_other = refs
    (above, below, held, winds, near_up, near_down, pass_up, pass_down, edge_state, edge_pass, edge_north, first_pass,
     moving, moving_north, beside_map, east, north, kappa, ratio, sems) = scratch
    count = LEVELS * FIELDS
    per_level = FIELDS * ROWS
    batches = LEVELS // BATCH
    copies = [
        pltpu.make_async_copy(
            state.at[pl.ds(n * BATCH, BATCH), pl.ds(begin * ROWS, SLICE), :],
            held.at[pl.ds(1 + n * BATCH, BATCH)],
            sems.at[n],
        )
        for n in range(batches)
    ]
    planes = ((far_east_wind, east), (far_north, north), (far_kappa, kappa))
    later = [pltpu.make_async_copy(there, here, sems.at[batches + n]) for n, (there, here) in enumerate(planes)]
    for copy in [later[0]] + copies + later[1:]:
        copy.start()
    each_start()

    @pl.when(is_odd("gx"))
    def _():
        above[...] = rows_partner[...]
        below[...] = rows_other[...]

    @pl.when(~is_odd("gx"))
    def _():
        above[...] = rows_other[...]
        below[...] = rows_partner[...]

    beside_map[...] = beside_matrix()
    spread_winds(winds, above, below)
    kinds = KINDS * LEVELS
    near_up[0:kinds, :] = above[begin * LEVELS : begin * LEVELS + kinds, :].astype(F32)
    near_up[kinds : kinds + 8, :] = jnp.zeros((8, COLS), F32)
    near_down[0:8, :] = jnp.zeros((8, COLS), F32)
    near_down[8 : kinds + 8, :] = below[begin * LEVELS : begin * LEVELS + kinds, :].astype(F32)
    pass_up[kinds : kinds + 8, :] = jnp.zeros((8, COLS), F32)
    pass_down[0:8, :] = jnp.zeros((8, COLS), F32)
    last_row, last_col = at_end("gx"), at_end("gy")
    row16 = lax.broadcasted_iota(jnp.int32, (ROWS, COLS), 0)
    lane16 = lanes((ROWS, COLS))
    row8 = lax.broadcasted_iota(jnp.int32, (8, COLS), 0)
    group = lanes((ROWS, COLS)) // 4

    def packed(start, size):
        kind = lanes((size, COLS)) % 4
        partner, other = from_partner[start : start + size, :].astype(F32), from_other[start : start + size, :].astype(F32)
        theirs = jnp.where((kind < 2) == is_odd("gy"), partner, other)
        return own[start : start + size, :], theirs

    def shifted(centre, first, last):
        up = jnp.where(row16 == 0, first, pltpu.roll(centre, 1, 0))
        if last is None:
            return up, None
        return up, jnp.where(row16 == ROWS - 1, last, pltpu.roll(centre, ROWS - 1, 0))

    _, rows_first = packed(2 * per_level + 4 * ROWS, 16)
    _, rows_last = packed(2 * per_level + 4 * ROWS + 16, 16)
    _, rows_wind = packed(2 * per_level + 4 * ROWS + 32, 16)
    strip_map = strip_matrix()
    _, east_edges = packed(2 * per_level, 2 * ROWS)
    own_north, north_edges = packed(2 * per_level + 2 * ROWS, 2 * ROWS)
    edge_north[...] = north_edges
    norths = dot(jnp.concatenate([north_edges.astype(BF16), own_north], axis=1), strip_map)
    for b in range(2):
        here = slice(b * ROWS, (b + 1) * ROWS)
        east_up, _ = shifted(east_edges[here], rows_wind[8 * b : 8 * b + 1, :], None)
        coefs = coefficients(east_up, east_edges[here], norths[here, :COLS], north_edges[here])
        mine, theirs = packed(b * per_level + begin * ROWS, SLICE)
        sides = dot(jnp.concatenate([theirs.astype(BF16), mine], axis=1), strip_map)
        for f in range(KINDS):
            part = slice(f * ROWS, (f + 1) * ROWS)
            n = 8 * b + begin + f
            up, down = shifted(theirs[part], rows_first[n : n + 1, :], rows_last[n : n + 1, :])
            at = b * SLICE + f * ROWS
            edge_state[at : at + ROWS, :] = theirs[part]
            edge_pass[at : at + ROWS, :] = combine(coefs, theirs[part], up, down, sides[part, :COLS], sides[part, COLS:])

    later[0].wait()
    for copy in copies:
        copy.wait()
    flat = held.reshape((LEVELS + 2) * SLICE, COLS)

    place = lax.broadcasted_iota(jnp.int32, (LEVELS, COLS), 0)
    at_level = lanes((LEVELS, COLS)) // 4 == place % HALF
    upper = place < HALF

    def spread(rows, n):
        value = jnp.where(upper, rows[n : n + 1, :], rows[8 + n : 9 + n, :])
        return jnp.where(at_level, value, 0.0).astype(BF16)

    def sides_of(values, halo):
        both = jnp.concatenate([values, halo], axis=1)
        return dot(both, beside_map[...])

    def wind_of(kind):
        return winds[kind * LEVELS : (kind + 1) * LEVELS, :]

    def strip(near, far, inner, out, offset, east_before, east_after, north_kind, corner, outward):
        north_here = wind_of(north_kind)
        north_left = sides_of(north_here.astype(BF16), spread(rows_wind, north_kind))[:, :COLS]
        coefs = coefficients(east_before, east_after, north_left, north_here)
        for f in range(KINDS):
            values = near[(begin + f) * LEVELS : (begin + f + 1) * LEVELS, :]
            sides = sides_of(values, spread(corner, begin + f))
            beyond = far[count + (begin + f) * LEVELS : count + (begin + f + 1) * LEVELS, :].astype(F32)
            within = flat[pl.ds(SLICE + f * ROWS + inner, LEVELS, stride=SLICE), :]
            up, down = (beyond, within) if outward else (within, beyond)
            at = offset + f * LEVELS
            out[at : at + LEVELS, :] = combine(coefs, values.astype(F32), up, down, sides[:, :COLS], sides[:, COLS:])

    strip(above, above, 0, pass_up, 0, wind_of(1), wind_of(0), 2, rows_first, True)
    own_last = jnp.where(last_row, 0.0, east[pl.ds(ROWS - 1, LEVELS, stride=ROWS), :])
    strip(below, below, ROWS - 1, pass_down, 8, own_last, wind_of(3), 4, rows_last, False)

    for copy in later[1:]:
        copy.wait()

    def load(moving, at, values, edge, number):
        size = values.shape[0]
        mine = lanes((size, COLS)) // 4 == number
        moving[at : at + size, 0:COLS] = values.astype(BF16)
        moving[at : at + size, COLS : 2 * COLS] = jnp.where(mine, edge, 0.0).astype(BF16)

    def one_batch(step, carried):
        previous, coupling, factor = carried
        b = step // (batches // 2)
        edge_at = pl.ds(pl.multiple_of(b * SLICE, SLICE), SLICE)
        north_at = pl.ds(pl.multiple_of(b * ROWS, ROWS), ROWS)
        first_number = (step % (batches // 2)) * BATCH
        norths = []
        for j in range(BATCH):
            level = step * BATCH + j
            here = flat[pl.ds(pl.multiple_of((level + 1) * SLICE, SLICE), SLICE), :]
            load(moving, j * SLICE, here, edge_state[edge_at, :], first_number + j)
            north_here = north[pl.ds(pl.multiple_of(level * ROWS, ROWS), ROWS), :]
            north_here = jnp.where((lane16 == COLS - 1) & last_col, 0.0, north_here)
            norths.append(north_here)
            load(moving_north, j * ROWS, north_here, edge_north[north_at, :], first_number + j)
        north_left = dot(moving_north[...], beside_map[:, 0:COLS])
        sides = dot(moving[...], beside_map[...])
        coefs = []
        for j in range(BATCH):
            level = step * BATCH + j
            at16 = pl.ds(pl.multiple_of(level * ROWS, ROWS), ROWS)
            east_here = jnp.where((row16 == ROWS - 1) & last_row, 0.0, east[at16, :])
            east_up = jnp.where(row16 == 0, winds[pl.ds(level, 1), :], pltpu.roll(east_here, 1, 0))
            coefs.append(coefficients(east_up, east_here, north_left[j * ROWS : (j + 1) * ROWS], norths[j]))

        def stencil(source, offset, j, level, first, last):
            found = []
            for f in range(KINDS):
                at = offset + f * ROWS
                line = f * LEVELS + level
                place = j * SLICE + f * ROWS
                for half in range(2):
                    r = at + 8 * half
                    here = source[pl.ds(pl.multiple_of(r, 8), 8), :]
                    up = source[pl.ds(r - 1, 8), :]
                    down = source[pl.ds(r + 1, 8), :]
                    if half == 0:
                        up = jnp.where(row8 == 0, first[pl.ds(line, 8), :], up)
                    else:
                        down = jnp.where(row8 == 7, last[pl.ds(line + 1, 8), :], down)
                    part = slice(place + 8 * half, place + 8 * half + 8)
                    mine = tuple(c[8 * half : 8 * half + 8] for c in coefs[j])
                    found.append(combine(mine, here, up, down, sides[part, :COLS], sides[part, COLS:]))
            return jnp.concatenate(found, axis=0)

        for j in range(BATCH):
            level = step * BATCH + j
            value = stencil(flat, (level + 1) * SLICE, j, level, near_up, near_down)
            first_pass[8 + j * SLICE : 8 + (j + 1) * SLICE, :] = value
            load(moving, j * SLICE, value, edge_pass[edge_at, :], first_number + j)
        sides = dot(moving[...], beside_map[...])
        for j in range(BATCH):
            level = step * BATCH + j
            value = stencil(first_pass, 8 + j * SLICE, j, level, pass_up, pass_down)
            at16 = pl.ds(pl.multiple_of(level * ROWS, ROWS), ROWS)
            next_at = pl.ds(pl.multiple_of(jnp.minimum(level, LEVELS - 2) * ROWS, ROWS), ROWS)
            next_coupling = jnp.where(level == LEVELS - 1, 0.0, kappa[next_at, :])
            flipped = 1.0 / (1.0 + coupling + next_coupling - coupling * factor)
            keep = coupling * flipped
            factor = next_coupling * flipped
            ratio[at16, :] = factor
            coupling = next_coupling
            after = []
            for f in range(KINDS):
                rhs = value[f * ROWS : (f + 1) * ROWS] * flipped + keep * previous[f]
                flat[pl.ds(pl.multiple_of((level + 1) * SLICE + f * ROWS, ROWS), ROWS), :] = rhs
                after.append(rhs)
            previous = tuple(after)
        return previous, coupling, factor

    start = tuple(jnp.zeros((ROWS, COLS), F32) for _ in range(KINDS))
    first_pass[0:8, :] = jnp.zeros((8, COLS), F32)
    first_pass[8 + BATCH * SLICE : 16 + BATCH * SLICE, :] = jnp.zeros((8, COLS), F32)
    zero = jnp.zeros((ROWS, COLS), F32)
    lax.fori_loop(0, batches, one_batch, (start, zero, zero))

    found = start
    for n in reversed(range(batches)):

        def upward(step, found):
            level = (n + 1) * BATCH - 1 - step
            factor = ratio[pl.ds(pl.multiple_of(level * ROWS, ROWS), ROWS), :]
            after = []
            for f in range(KINDS):
                here = pl.ds(pl.multiple_of((level + 1) * SLICE + f * ROWS, ROWS), ROWS)
                value = flat[here, :] + factor * found[f]
                flat[here, :] = value
                after.append(value)
            return tuple(after)

        found = lax.fori_loop(0, BATCH, upward, found, unroll=UNROLL)
        each_batch(n)


def advance_scratch():
    rows = LEVELS * KINDS + 8
    return [
        pltpu.VMEM((ROW_MESSAGE, COLS), BF16),
        pltpu.VMEM((ROW_MESSAGE, COLS), BF16),
        pltpu.VMEM((LEVELS + 2, SLICE, COLS), F32),
        pltpu.VMEM((8 * LEVELS, COLS), F32),
        pltpu.VMEM((rows, COLS), F32),
        pltpu.VMEM((rows, COLS), F32),
        pltpu.VMEM((rows, COLS), F32),
        pltpu.VMEM((rows, COLS), F32),
        pltpu.VMEM((2 * SLICE, COLS), F32),
        pltpu.VMEM((2 * SLICE, COLS), F32),
        pltpu.VMEM((2 * ROWS, COLS), F32),
        pltpu.VMEM((16 + BATCH * SLICE, COLS), F32),
        pltpu.VMEM((BATCH * SLICE, 2 * COLS), BF16),
        pltpu.VMEM((BATCH * ROWS, 2 * COLS), BF16),
        pltpu.VMEM((2 * COLS, 2 * COLS), BF16),
        pltpu.VMEM((LEVELS * ROWS, COLS), F32),
        pltpu.VMEM((LEVELS * ROWS, COLS), F32),
        pltpu.VMEM(((LEVELS - 1) * ROWS, COLS), F32),
        pltpu.VMEM((LEVELS * ROWS, COLS), F32),
        pltpu.SemaphoreType.DMA((LEVELS // BATCH + 3,)),
    ]


def sigmoid(values):
    return 0.5 * jnp.tanh(0.5 * values) + 0.5


def dot(left, right):
    return jnp.dot(left, right, preferred_element_type=F32)


def dot_last(left, right):
    return lax.dot_general(left, right, (((1,), (1,)), ((), ())), preferred_element_type=F32)


GROUP = 8


def main_kernel(*refs):
    ins, far, (solved, far_adjoint, far_active) = refs[:9], refs[9:15], refs[15:18]
    near, (adjoint, active, sems), scratch = refs[18:24], refs[24:27], refs[27:]
    held = scratch[2]
    fetches = [pltpu.make_async_copy(there, here, sems.at[n]) for n, (there, here) in enumerate(zip(far, near))]
    cotan, w_in_t, w_mid_t, w_out, w_mid, w_in = near
    copies = [
        pltpu.make_async_copy(
            held.at[pl.ds(1 + n * BATCH, BATCH)], solved.at[pl.ds(n * BATCH, BATCH)], sems.at[6 + n]
        )
        for n in range(LEVELS // BATCH)
    ]

    def begin():
        for fetch in fetches:
            fetch.start()

    advance(0, ins, begin, lambda n: copies[n].start(), scratch)
    for fetch in fetches:
        fetch.wait()
    lines = held.reshape((LEVELS + 2) * SLICE, COLS)
    to_slab = ones_where((COLS, COLS), lambda row, col: row == (col % 16) * 8 + col // 16)
    to_physics = ones_where((COLS, COLS), lambda row, col: col == (row % 16) * 8 + row // 16)
    sends = []
    for step in range(ROWS // GROUP):
        rows = [GROUP * step + k for k in range(GROUP)]
        parts = [lines[pl.ds(SLICE + r, FEATURES, stride=ROWS), :].astype(BF16) for r in rows]
        inputs = jnp.concatenate(parts, axis=1)
        first = dot(w_in_t[...], inputs)
        gate = sigmoid(first)
        value = first * gate
        slope_one = gate * (1.0 + first - value)
        second = dot(w_mid_t[...], value.astype(BF16))
        gate = sigmoid(second)
        value = second * gate
        slope_two = gate * (1.0 + second - value)
        here = pl.ds(step * HIDDEN, HIDDEN)
        active[here, :] = value.astype(BF16)
        sends.append(pltpu.make_async_copy(active.at[here], far_active.at[here], sems.at[10 + 2 * step]))
        sends[-1].start()
        blocks = [slice(r * COLS, (r + 1) * COLS) for r in rows]
        moved = jnp.concatenate([dot(to_slab, cotan[at, :]).astype(BF16) for at in blocks], axis=0)
        delta_two = (dot_last(w_out[...], moved) * slope_two).astype(BF16)
        delta_one = (dot(w_mid[...], delta_two) * slope_one).astype(BF16)
        back = dot(w_in[...], delta_one).astype(BF16)
        for k, at in enumerate(blocks):
            adjoint[at, :] = dot_last(to_physics, back[:, k * COLS : (k + 1) * COLS]).astype(BF16)
        here = pl.ds(step * GROUP * COLS, GROUP * COLS)
        sends.append(pltpu.make_async_copy(adjoint.at[here], far_adjoint.at[here], sems.at[11 + 2 * step]))
        sends[-1].start()
    for copy in copies + sends:
        copy.wait()


def last_kernel(*refs):
    ins, (solved, active, w_out_t), out, (mixed, sems), scratch = refs[:9], refs[9:12], refs[12], refs[13:15], refs[15:]
    held = scratch[2]
    batches = LEVELS // BATCH
    fetch = pltpu.make_async_copy(solved, mixed, sems.at[batches + 1])
    fetch.start()
    lines = mixed.reshape(LEVELS * SLICE, COLS)
    for step in range(ROWS // GROUP):
        tend = dot(w_out_t[...], active[step * HIDDEN : (step + 1) * HIDDEN, :])
        tend = tend.astype(BF16).astype(F32)
        if step == 0:
            fetch.wait()
        for k in range(GROUP):
            here = pl.ds(GROUP * step + k, FEATURES, stride=ROWS)
            lines[here, :] = lines[here, :] + tend[:, k * COLS : (k + 1) * COLS]
    first = pltpu.make_async_copy(mixed, out.at[:, pl.ds(0, SLICE), :], sems.at[batches])
    first.start()
    copies = [
        pltpu.make_async_copy(
            held.at[pl.ds(1 + n * BATCH, BATCH)],
            out.at[pl.ds(n * BATCH, BATCH), pl.ds(SLICE, SLICE), :],
            sems.at[n],
        )
        for n in range(batches)
    ]
    advance(KINDS, ins, lambda: None, lambda n: copies[n].start(), scratch)
    first.wait()
    for copy in copies:
        copy.wait()


def run(kernel, outs, scratch, flops, moved, *args, name=None, far=(), limit=62914560, **rest):
    anywhere, near = pl.BlockSpec(memory_space=pl.ANY), pl.BlockSpec(memory_space=pltpu.VMEM)
    rest = rest or dict(in_specs=[anywhere if n in far else near for n in range(len(args))])
    return pl.pallas_call(
        kernel,
        out_shape=[jax.ShapeDtypeStruct(shape, kind) for shape, kind in outs],
        scratch_shapes=scratch,
        compiler_params=pltpu.CompilerParams(vmem_limit_bytes=limit),
        cost_estimate=pl.CostEstimate(flops=flops, bytes_accessed=moved, transcendentals=0),
        name=name,
        **rest,
    )(*args)


FAR = (0, 1, 2, 3)


def main(ins, cotan, *weights):
    near = pl.BlockSpec(memory_space=pltpu.VMEM)
    far = pl.BlockSpec(memory_space=pl.ANY)
    outs = [
        ((LEVELS, SLICE, COLS), F32),
        ((ROWS * COLS, FEATURES), BF16),
        ((ROWS // GROUP * HIDDEN, GROUP * COLS), BF16),
    ]
    held = [pltpu.VMEM(x.shape, BF16) for x in (cotan,) + weights]
    held += [pltpu.VMEM(*outs[1]), pltpu.VMEM(*outs[2]), pltpu.SemaphoreType.DMA((10 + 2 * ROWS // GROUP,))]
    return run(
        main_kernel, outs, held + advance_scratch(), 4 * 10**9, 10**7, *ins, cotan, *weights, name="main",
        in_specs=[far if n in FAR or n >= 9 else near for n in range(15)], out_specs=[far] * 3,
    )


def last(ins, solved, active, w_out_t):
    near = pl.BlockSpec(memory_space=pltpu.VMEM)
    far = pl.BlockSpec(memory_space=pl.ANY)
    mixed = [pltpu.VMEM((LEVELS, SLICE, COLS), F32), pltpu.SemaphoreType.DMA((LEVELS // BATCH + 2,))]
    (new_state,) = run(
        last_kernel, [((LEVELS, FIELDS * ROWS, COLS), F32)], mixed + advance_scratch(), 10**9, 2 * 10**7,
        *ins, solved, active, w_out_t, name="last_fields",
        in_specs=[far if n in FAR + (9,) else near for n in range(12)], out_specs=[far],
    )
    return new_state


def swap(block, axis, start):
    firsts = range(start, lax.axis_size(axis) - 1, 2)
    return lax.ppermute(block, axis, [(i, i + 1) for i in firsts] + [(i + 1, i) for i in firsts])


def exchange(blocks):
    return lax.all_to_all(blocks, ("gx", "gy"), split_axis=0, concat_axis=0, tiled=True)


def shards(state, east_wind, north_wind, kappa, w_in, w_mid, w_out, cotangent):
    devices = lax.axis_size("gx") * lax.axis_size("gy")
    flat = state.reshape(LEVELS * FIELDS * ROWS, COLS)
    east = east_wind.reshape(LEVELS * ROWS, COLS)
    north = north_wind.reshape(LEVELS * ROWS, COLS)
    message = ((ROW_MESSAGE, COLS), BF16)
    to_partner, to_other = run(rows_kernel, [message, message], [], 10**6, 5 * 10**6, flat, east, north, name="rows")
    arrived = exchange(cotangent.reshape(devices, ROWS * COLS // devices, FEATURES))
    from_other = swap(to_other, "gx", 1)
    from_partner = swap(to_partner, "gx", 0)
    count = LEVELS * FIELDS
    flipped = [(w.shape[::-1], BF16) for w in (w_in, w_mid, w_out)]
    edges, w_in_t, w_mid_t, w_out_t = run(
        cols_kernel, [((COL_MESSAGE - 48, COLS), BF16)] + flipped, [], 10**8, 10**7,
        flat, east, north, w_in, w_mid, w_out, name="cols",
    )
    (own,) = run(
        corners_kernel, [((COL_MESSAGE, COLS), BF16)], [pltpu.VMEM((count, COLS), BF16)], 10**6, 10**6,
        edges, from_partner, from_other, name="corners", limit=8 * 1024 * 1024,
    )
    rows_partner, rows_other = from_partner, from_other
    from_other = swap(own, "gy", 1)
    from_partner = swap(own, "gy", 0)
    ins = (state.reshape(LEVELS, FIELDS * ROWS, COLS), east, north, kappa.reshape((LEVELS - 1) * ROWS, COLS))
    ins += (rows_partner, rows_other, own, from_partner, from_other)
    cotan = arrived.reshape(ROWS * COLS, FEATURES)
    solved, adjoint, active = main(ins, cotan, w_in_t, w_mid_t, w_out, w_mid, w_in)
    returned = exchange(adjoint.reshape(devices, ROWS * COLS // devices, FEATURES))
    new_state = last(ins, solved, active, w_out_t)
    return new_state.reshape(state.shape), returned.reshape(ROWS * COLS, FEATURES)


def solution(mesh):
    in_specs = (
        P(None, None, "gx", "gy"),
        P(None, "gx", "gy"),
        P(None, "gx", "gy"),
        P(None, "gx", "gy"),
        P(),
        P(),
        P(),
        P(("gx", "gy"), None),
    )
    out_specs = (P(None, None, "gx", "gy"), P(("gx", "gy"), None))
    return jax.shard_map(shards, mesh=mesh, in_specs=in_specs, out_specs=out_specs, check_vma=False)
```

```python
import functools

import jax
import jax.numpy as jnp
from jax import lax
from jax.experimental import pallas as pl
from jax.experimental.pallas import tpu as pltpu
from jax.sharding import PartitionSpec as P

F32 = jnp.float32
BF16 = jnp.bfloat16
LEVELS, FIELDS, ROWS, COLS = 64, 8, 16, 128
KINDS = 4
HIDDEN, FEATURES = 512, 256
HALF = LEVELS // 2
ROW_MESSAGE = 2 * LEVELS * FIELDS + 3 * LEVELS
COL_MESSAGE = 2 * (FIELDS * ROWS + 2 * ROWS + 3 * FIELDS)
UNROLL = 4


def at_end(axis):
    return lax.axis_index(axis) == lax.axis_size(axis) - 1


def lanes(shape):
    return lax.broadcasted_iota(jnp.int32, shape, len(shape) - 1)


def is_odd(axis):
    return lax.axis_index(axis) % 2 == 1


def rows_kernel(state, east, north, partner, other):
    closed = (lanes((LEVELS, COLS)) == COLS - 1) & at_end("gy")
    count = LEVELS * FIELDS

    def fill(out, near, far):
        for f in range(FIELDS):
            at = f * LEVELS
            out[at : at + LEVELS, :] = state[pl.ds(f * ROWS + near, LEVELS, stride=FIELDS * ROWS), :].astype(BF16)
            at += count
            out[at : at + LEVELS, :] = state[pl.ds(f * ROWS + far, LEVELS, stride=FIELDS * ROWS), :].astype(BF16)
        base = 2 * count
        out[base : base + LEVELS, :] = east[pl.ds(near, LEVELS, stride=ROWS), :].astype(BF16)
        out[base + LEVELS : base + 2 * LEVELS, :] = east[pl.ds(far, LEVELS, stride=ROWS), :].astype(BF16)
        north_near = north[pl.ds(near, LEVELS, stride=ROWS), :]
        out[base + 2 * LEVELS : base + 3 * LEVELS, :] = jnp.where(closed, 0.0, north_near).astype(BF16)

    @pl.when(is_odd("gx"))
    def _():
        fill(partner, 0, 1)
        fill(other, ROWS - 1, ROWS - 2)

    @pl.when(~is_odd("gx"))
    def _():
        fill(partner, ROWS - 1, ROWS - 2)
        fill(other, 0, 1)


def spread_winds(winds, above, below):
    base = 2 * LEVELS * FIELDS
    winds[0 : 3 * LEVELS, :] = above[base : base + 3 * LEVELS, :].astype(winds.dtype)
    winds[3 * LEVELS : 4 * LEVELS, :] = below[base : base + LEVELS, :].astype(winds.dtype)
    winds[4 * LEVELS : 5 * LEVELS, :] = below[base + 2 * LEVELS : base + 3 * LEVELS, :].astype(winds.dtype)
    winds[5 * LEVELS : 8 * LEVELS, :] = jnp.zeros((3 * LEVELS, COLS), winds.dtype)


def ones_where(shape, rule):
    row = lax.broadcasted_iota(jnp.int32, shape, 0)
    col = lax.broadcasted_iota(jnp.int32, shape, 1)
    return jnp.where(rule(row, col), 1.0, 0.0).astype(BF16)


def edge_matrix():
    return ones_where((COLS, COLS), lambda row, col: (row + 2) % COLS == col % 4)


def cols_kernel(state, east, north, w_in, w_mid, w_out, out, *prepared):
    prepare(w_in, w_mid, w_out, *prepared)
    per_level = FIELDS * ROWS
    gather = edge_matrix()
    row = lax.broadcasted_iota(jnp.int32, (ROWS, COLS), 0)
    lane = lanes((ROWS, COLS))
    many = 16
    for b in range(2):

        def body(step, totals):
            level = b * HALF + step * many
            merged = list(totals)
            for n, (ref, size) in enumerate(((state, per_level), (east, ROWS), (north, ROWS))):
                at = pl.ds(pl.multiple_of(level * size, size), many * size)
                edges = dot(ref[at, :].astype(BF16), gather)
                for k in range(many):
                    mine = (lanes((size, COLS)) // 4) == step * many + k
                    merged[n] = jnp.where(mine, edges[k * size : (k + 1) * size], merged[n])
            return tuple(merged)

        start = tuple(jnp.zeros((n, COLS), F32) for n in (per_level, ROWS, ROWS))
        fields, east_edge, north_edge = lax.fori_loop(0, HALF // many, body, start)
        east_edge = jnp.where((row == ROWS - 1) & at_end("gx"), 0.0, east_edge)
        north_edge = jnp.where((lane % 4 == 1) & at_end("gy"), 0.0, north_edge)
        out[b * per_level : (b + 1) * per_level, :] = fields.astype(BF16)
        base = 2 * per_level
        out[base + b * ROWS : base + (b + 1) * ROWS, :] = east_edge.astype(BF16)
        base += 2 * ROWS
        out[base + b * ROWS : base + (b + 1) * ROWS, :] = north_edge.astype(BF16)


def corners_kernel(edges, from_partner, from_other, out, winds):
    @pl.when(is_odd("gx"))
    def _():
        corners(edges, from_partner, from_other, out, winds)

    @pl.when(~is_odd("gx"))
    def _():
        corners(edges, from_other, from_partner, out, winds)


def corners(edges, above, below, out, winds):
    count = LEVELS * FIELDS
    spread_winds(winds, above, below)
    gather = edge_matrix()
    collect = ones_where(
        (16, count), lambda row, col: (row % 8 == col // LEVELS) & (row // 8 == (col % LEVELS) // HALF)
    )
    level = lax.broadcasted_iota(jnp.int32, (count, COLS), 0) % HALF
    mine = lanes((count, COLS)) // 4 == level
    size = edges.shape[0]
    out[0:size, :] = edges[...]
    for n, source in enumerate((above[0:count, :], below[0:count, :], winds[...])):
        spread = jnp.where(mine, dot(source, gather), 0.0).astype(BF16)
        out[size + 16 * n : size + 16 * (n + 1), :] = dot(collect, spread).astype(BF16)


def prepare(w_in, w_mid, w_out, w_in_t, w_mid_t, w_out_t):
    by_level = ones_where(
        (FEATURES, FEATURES), lambda row, col: row == (col % KINDS) * LEVELS + col // KINDS
    )
    w_in_t[...] = dot(w_in[...].T, by_level).astype(BF16)
    w_mid_t[...] = w_mid[...].T
    w_out_t[...] = dot(w_out[...], by_level).astype(BF16).T


def coefficients(east_up, east, north_left, north):
    zero = 0.0
    east_plus, east_minus = jnp.maximum(east_up, zero), jnp.minimum(east, zero)
    north_plus, north_minus = jnp.maximum(north_left, zero), jnp.minimum(north, zero)
    centre = (
        1.0
        - (jnp.maximum(east, zero) - jnp.minimum(east_up, zero))
        - (jnp.maximum(north, zero) - jnp.minimum(north_left, zero))
    )
    return centre, east_plus, -east_minus, north_plus, -north_minus


def combine(coefs, here, up, down, left, right):
    centre, from_up, from_down, from_left, from_right = coefs
    return centre * here + (from_up * up + from_down * down) + (from_left * left + from_right * right)


def beside_matrix():
    def rule(row, col):
        lane, place = row % COLS, col % COLS
        inside = either(col < COLS, lane + 1 == place, lane == place + 1)
        halo = either(col < COLS, (place == 0) & (lane % 4 == 1), (place == COLS - 1) & (lane % 4 == 2))
        return either(row < COLS, inside, halo)

    return ones_where((2 * COLS, 2 * COLS), rule)


def strip_matrix():
    def rule(row, col):
        lane, place = row % COLS, col % COLS
        theirs = row < COLS
        one, two = place % 4 == 1, place % 4 == 2
        left = (lane + 1 == place) & either(theirs, one, two)
        right = (lane == place + 1) & either(theirs, two, one)
        return either(col < COLS, left, right)

    return ones_where((2 * COLS, 2 * COLS), rule)


def either(choice, yes, no):
    return (choice & yes) | (~choice & no)


BATCH = 32
SLICE = KINDS * ROWS


def advance(begin, refs, each_start, each_batch, scratch):
    state, far_east_wind, far_north, far_kappa, rows_partner, rows_other, own, from_partner, from_other = refs
    (above, below, held, winds, near_up, near_down, pass_up, pass_down, edge_state, edge_pass, edge_north, first_pass,
     moving, moving_north, beside_map, east, north, kappa, ratio, sems) = scratch
    count = LEVELS * FIELDS
    per_level = FIELDS * ROWS
    batches = LEVELS // BATCH
    copies = [
        pltpu.make_async_copy(
            state.at[pl.ds(n * BATCH, BATCH), pl.ds(begin * ROWS, SLICE), :],
            held.at[pl.ds(1 + n * BATCH, BATCH)],
            sems.at[n],
        )
        for n in range(batches)
    ]
    planes = ((far_east_wind, east), (far_north, north), (far_kappa, kappa))
    later = [pltpu.make_async_copy(there, here, sems.at[batches + n]) for n, (there, here) in enumerate(planes)]
    for copy in [later[0]] + copies + later[1:]:
        copy.start()
    each_start()

    @pl.when(is_odd("gx"))
    def _():
        above[...] = rows_partner[...]
        below[...] = rows_other[...]

    @pl.when(~is_odd("gx"))
    def _():
        above[...] = rows_other[...]
        below[...] = rows_partner[...]

    beside_map[...] = beside_matrix()
    spread_winds(winds, above, below)
    kinds = KINDS * LEVELS
    near_up[0:kinds, :] = above[begin * LEVELS : begin * LEVELS + kinds, :].astype(F32)
    near_up[kinds : kinds + 8, :] = jnp.zeros((8, COLS), F32)
    near_down[0:8, :] = jnp.zeros((8, COLS), F32)
    near_down[8 : kinds + 8, :] = below[begin * LEVELS : begin * LEVELS + kinds, :].astype(F32)
    pass_up[kinds : kinds + 8, :] = jnp.zeros((8, COLS), F32)
    pass_down[0:8, :] = jnp.zeros((8, COLS), F32)
    last_row, last_col = at_end("gx"), at_end("gy")
    row16 = lax.broadcasted_iota(jnp.int32, (ROWS, COLS), 0)
    lane16 = lanes((ROWS, COLS))
    row8 = lax.broadcasted_iota(jnp.int32, (8, COLS), 0)
    group = lanes((ROWS, COLS)) // 4

    def packed(start, size):
        kind = lanes((size, COLS)) % 4
        partner, other = from_partner[start : start + size, :].astype(F32), from_other[start : start + size, :].astype(F32)
        theirs = jnp.where((kind < 2) == is_odd("gy"), partner, other)
        return own[start : start + size, :], theirs

    def shifted(centre, first, last):
        up = jnp.where(row16 == 0, first, pltpu.roll(centre, 1, 0))
        if last is None:
            return up, None
        return up, jnp.where(row16 == ROWS - 1, last, pltpu.roll(centre, ROWS - 1, 0))

    _, rows_first = packed(2 * per_level + 4 * ROWS, 16)
    _, rows_last = packed(2 * per_level + 4 * ROWS + 16, 16)
    _, rows_wind = packed(2 * per_level + 4 * ROWS + 32, 16)
    strip_map = strip_matrix()
    _, east_edges = packed(2 * per_level, 2 * ROWS)
    own_north, north_edges = packed(2 * per_level + 2 * ROWS, 2 * ROWS)
    edge_north[...] = north_edges
    norths = dot(jnp.concatenate([north_edges.astype(BF16), own_north], axis=1), strip_map)
    for b in range(2):
        here = slice(b * ROWS, (b + 1) * ROWS)
        east_up, _ = shifted(east_edges[here], rows_wind[8 * b : 8 * b + 1, :], None)
        coefs = coefficients(east_up, east_edges[here], norths[here, :COLS], north_edges[here])
        mine, theirs = packed(b * per_level + begin * ROWS, SLICE)
        sides = dot(jnp.concatenate([theirs.astype(BF16), mine], axis=1), strip_map)
        for f in range(KINDS):
            part = slice(f * ROWS, (f + 1) * ROWS)
            n = 8 * b + begin + f
            up, down = shifted(theirs[part], rows_first[n : n + 1, :], rows_last[n : n + 1, :])
            at = b * SLICE + f * ROWS
            edge_state[at : at + ROWS, :] = theirs[part]
            edge_pass[at : at + ROWS, :] = combine(coefs, theirs[part], up, down, sides[part, :COLS], sides[part, COLS:])

    later[0].wait()
    for copy in copies:
        copy.wait()
    flat = held.reshape((LEVELS + 2) * SLICE, COLS)

    place = lax.broadcasted_iota(jnp.int32, (LEVELS, COLS), 0)
    at_level = lanes((LEVELS, COLS)) // 4 == place % HALF
    upper = place < HALF

    def spread(rows, n):
        value = jnp.where(upper, rows[n : n + 1, :], rows[8 + n : 9 + n, :])
        return jnp.where(at_level, value, 0.0).astype(BF16)

    def sides_of(values, halo):
        both = jnp.concatenate([values, halo], axis=1)
        return dot(both, beside_map[...])

    def wind_of(kind):
        return winds[kind * LEVELS : (kind + 1) * LEVELS, :]

    def strip(near, far, inner, out, offset, east_before, east_after, north_kind, corner, outward):
        north_here = wind_of(north_kind)
        north_left = sides_of(north_here.astype(BF16), spread(rows_wind, north_kind))[:, :COLS]
        coefs = coefficients(east_before, east_after, north_left, north_here)
        for f in range(KINDS):
            values = near[(begin + f) * LEVELS : (begin + f + 1) * LEVELS, :]
            sides = sides_of(values, spread(corner, begin + f))
            beyond = far[count + (begin + f) * LEVELS : count + (begin + f + 1) * LEVELS, :].astype(F32)
            within = flat[pl.ds(SLICE + f * ROWS + inner, LEVELS, stride=SLICE), :]
            up, down = (beyond, within) if outward else (within, beyond)
            at = offset + f * LEVELS
            out[at : at + LEVELS, :] = combine(coefs, values.astype(F32), up, down, sides[:, :COLS], sides[:, COLS:])

    strip(above, above, 0, pass_up, 0, wind_of(1), wind_of(0), 2, rows_first, True)
    own_last = jnp.where(last_row, 0.0, east[pl.ds(ROWS - 1, LEVELS, stride=ROWS), :])
    strip(below, below, ROWS - 1, pass_down, 8, own_last, wind_of(3), 4, rows_last, False)

    for copy in later[1:]:
        copy.wait()

    def load(moving, at, values, edge, number):
        size = values.shape[0]
        mine = lanes((size, COLS)) // 4 == number
        moving[at : at + size, 0:COLS] = values.astype(BF16)
        moving[at : at + size, COLS : 2 * COLS] = jnp.where(mine, edge, 0.0).astype(BF16)

    def one_batch(step, carried):
        previous, coupling, factor = carried
        b = step // (batches // 2)
        edge_at = pl.ds(pl.multiple_of(b * SLICE, SLICE), SLICE)
        north_at = pl.ds(pl.multiple_of(b * ROWS, ROWS), ROWS)
        first_number = (step % (batches // 2)) * BATCH
        norths = []
        for j in range(BATCH):
            level = step * BATCH + j
            here = flat[pl.ds(pl.multiple_of((level + 1) * SLICE, SLICE), SLICE), :]
            load(moving, j * SLICE, here, edge_state[edge_at, :], first_number + j)
            north_here = north[pl.ds(pl.multiple_of(level * ROWS, ROWS), ROWS), :]
            north_here = jnp.where((lane16 == COLS - 1) & last_col, 0.0, north_here)
            norths.append(north_here)
            load(moving_north, j * ROWS, north_here, edge_north[north_at, :], first_number + j)
        north_left = dot(moving_north[...], beside_map[:, 0:COLS])
        sides = dot(moving[...], beside_map[...])
        coefs = []
        for j in range(BATCH):
            level = step * BATCH + j
            at16 = pl.ds(pl.multiple_of(level * ROWS, ROWS), ROWS)
            east_here = jnp.where((row16 == ROWS - 1) & last_row, 0.0, east[at16, :])
            east_up = jnp.where(row16 == 0, winds[pl.ds(level, 1), :], pltpu.roll(east_here, 1, 0))
            coefs.append(coefficients(east_up, east_here, north_left[j * ROWS : (j + 1) * ROWS], norths[j]))

        def stencil(source, offset, j, level, first, last):
            found = []
            for f in range(KINDS):
                at = offset + f * ROWS
                line = f * LEVELS + level
                place = j * SLICE + f * ROWS
                for half in range(2):
                    r = at + 8 * half
                    here = source[pl.ds(pl.multiple_of(r, 8), 8), :]
                    up = source[pl.ds(r - 1, 8), :]
                    down = source[pl.ds(r + 1, 8), :]
                    if half == 0:
                        up = jnp.where(row8 == 0, first[pl.ds(line, 8), :], up)
                    else:
                        down = jnp.where(row8 == 7, last[pl.ds(line + 1, 8), :], down)
                    part = slice(place + 8 * half, place + 8 * half + 8)
                    mine = tuple(c[8 * half : 8 * half + 8] for c in coefs[j])
                    found.append(combine(mine, here, up, down, sides[part, :COLS], sides[part, COLS:]))
            return jnp.concatenate(found, axis=0)

        for j in range(BATCH):
            level = step * BATCH + j
            value = stencil(flat, (level + 1) * SLICE, j, level, near_up, near_down)
            first_pass[8 + j * SLICE : 8 + (j + 1) * SLICE, :] = value
            load(moving, j * SLICE, value, edge_pass[edge_at, :], first_number + j)
        sides = dot(moving[...], beside_map[...])
        for j in range(BATCH):
            level = step * BATCH + j
            value = stencil(first_pass, 8 + j * SLICE, j, level, pass_up, pass_down)
            at16 = pl.ds(pl.multiple_of(level * ROWS, ROWS), ROWS)
            next_at = pl.ds(pl.multiple_of(jnp.minimum(level, LEVELS - 2) * ROWS, ROWS), ROWS)
            next_coupling = jnp.where(level == LEVELS - 1, 0.0, kappa[next_at, :])
            flipped = 1.0 / (1.0 + coupling + next_coupling - coupling * factor)
            keep = coupling * flipped
            factor = next_coupling * flipped
            ratio[at16, :] = factor
            coupling = next_coupling
            after = []
            for f in range(KINDS):
                rhs = value[f * ROWS : (f + 1) * ROWS] * flipped + keep * previous[f]
                flat[pl.ds(pl.multiple_of((level + 1) * SLICE + f * ROWS, ROWS), ROWS), :] = rhs
                after.append(rhs)
            previous = tuple(after)
        return previous, coupling, factor

    start = tuple(jnp.zeros((ROWS, COLS), F32) for _ in range(KINDS))
    first_pass[0:8, :] = jnp.zeros((8, COLS), F32)
    first_pass[8 + BATCH * SLICE : 16 + BATCH * SLICE, :] = jnp.zeros((8, COLS), F32)
    zero = jnp.zeros((ROWS, COLS), F32)
    lax.fori_loop(0, batches, one_batch, (start, zero, zero))

    found = start
    for n in reversed(range(batches)):

        def upward(step, found):
            level = (n + 1) * BATCH - 1 - step
            factor = ratio[pl.ds(pl.multiple_of(level * ROWS, ROWS), ROWS), :]
            after = []
            for f in range(KINDS):
                here = pl.ds(pl.multiple_of((level + 1) * SLICE + f * ROWS, ROWS), ROWS)
                value = flat[here, :] + factor * found[f]
                flat[here, :] = value
                after.append(value)
            return tuple(after)

        found = lax.fori_loop(0, BATCH, upward, found, unroll=UNROLL)
        each_batch(n)


def advance_scratch():
    rows = LEVELS * KINDS + 8
    return [
        pltpu.VMEM((ROW_MESSAGE, COLS), BF16),
        pltpu.VMEM((ROW_MESSAGE, COLS), BF16),
        pltpu.VMEM((LEVELS + 2, SLICE, COLS), F32),
        pltpu.VMEM((8 * LEVELS, COLS), F32),
        pltpu.VMEM((rows, COLS), F32),
        pltpu.VMEM((rows, COLS), F32),
        pltpu.VMEM((rows, COLS), F32),
        pltpu.VMEM((rows, COLS), F32),
        pltpu.VMEM((2 * SLICE, COLS), F32),
        pltpu.VMEM((2 * SLICE, COLS), F32),
        pltpu.VMEM((2 * ROWS, COLS), F32),
        pltpu.VMEM((16 + BATCH * SLICE, COLS), F32),
        pltpu.VMEM((BATCH * SLICE, 2 * COLS), BF16),
        pltpu.VMEM((BATCH * ROWS, 2 * COLS), BF16),
        pltpu.VMEM((2 * COLS, 2 * COLS), BF16),
        pltpu.VMEM((LEVELS * ROWS, COLS), F32),
        pltpu.VMEM((LEVELS * ROWS, COLS), F32),
        pltpu.VMEM(((LEVELS - 1) * ROWS, COLS), F32),
        pltpu.VMEM((LEVELS * ROWS, COLS), F32),
        pltpu.SemaphoreType.DMA((LEVELS // BATCH + 3,)),
    ]


def sigmoid(values):
    return 0.5 * jnp.tanh(0.5 * values) + 0.5


def dot(left, right):
    return jnp.dot(left, right, preferred_element_type=F32)


def dot_last(left, right):
    return lax.dot_general(left, right, (((1,), (1,)), ((), ())), preferred_element_type=F32)


GROUP = 8


def main_kernel(*refs):
    ins, far, (solved, far_adjoint, far_active) = refs[:9], refs[9:15], refs[15:18]
    near, (adjoint, active, sems), scratch = refs[18:24], refs[24:27], refs[27:]
    held = scratch[2]
    fetches = [pltpu.make_async_copy(there, here, sems.at[n]) for n, (there, here) in enumerate(zip(far, near))]
    cotan, w_in_t, w_mid_t, w_out, w_mid, w_in = near
    copies = [
        pltpu.make_async_copy(
            held.at[pl.ds(1 + n * BATCH, BATCH)], solved.at[pl.ds(n * BATCH, BATCH)], sems.at[6 + n]
        )
        for n in range(LEVELS // BATCH)
    ]

    def begin():
        for fetch in fetches:
            fetch.start()

    advance(0, ins, begin, lambda n: copies[n].start(), scratch)
    for fetch in fetches:
        fetch.wait()
    lines = held.reshape((LEVELS + 2) * SLICE, COLS)
    to_slab = ones_where((COLS, COLS), lambda row, col: row == (col % 16) * 8 + col // 16)
    to_physics = ones_where((COLS, COLS), lambda row, col: col == (row % 16) * 8 + row // 16)
    sends = []
    for step in range(ROWS // GROUP):
        rows = [GROUP * step + k for k in range(GROUP)]
        parts = [lines[pl.ds(SLICE + r, FEATURES, stride=ROWS), :].astype(BF16) for r in rows]
        inputs = jnp.concatenate(parts, axis=1)
        first = dot(w_in_t[...], inputs)
        gate = sigmoid(first)
        value = first * gate
        slope_one = gate * (1.0 + first - value)
        second = dot(w_mid_t[...], value.astype(BF16))
        gate = sigmoid(second)
        value = second * gate
        slope_two = gate * (1.0 + second - value)
        here = pl.ds(step * HIDDEN, HIDDEN)
        active[here, :] = value.astype(BF16)
        sends.append(pltpu.make_async_copy(active.at[here], far_active.at[here], sems.at[10 + 2 * step]))
        sends[-1].start()
        blocks = [slice(r * COLS, (r + 1) * COLS) for r in rows]
        moved = jnp.concatenate([dot(to_slab, cotan[at, :]).astype(BF16) for at in blocks], axis=0)
        delta_two = (dot_last(w_out[...], moved) * slope_two).astype(BF16)
        delta_one = (dot(w_mid[...], delta_two) * slope_one).astype(BF16)
        back = dot(w_in[...], delta_one).astype(BF16)
        for k, at in enumerate(blocks):
            adjoint[at, :] = dot_last(to_physics, back[:, k * COLS : (k + 1) * COLS]).astype(BF16)
        here = pl.ds(step * GROUP * COLS, GROUP * COLS)
        sends.append(pltpu.make_async_copy(adjoint.at[here], far_adjoint.at[here], sems.at[11 + 2 * step]))
        sends[-1].start()
    for copy in copies + sends:
        copy.wait()


def last_kernel(*refs):
    ins, (solved, active, w_out_t), out, (mixed, sems), scratch = refs[:9], refs[9:12], refs[12], refs[13:15], refs[15:]
    held = scratch[2]
    batches = LEVELS // BATCH
    fetch = pltpu.make_async_copy(solved, mixed, sems.at[batches + 1])
    fetch.start()
    lines = mixed.reshape(LEVELS * SLICE, COLS)
    for step in range(ROWS // GROUP):
        tend = dot(w_out_t[...], active[step * HIDDEN : (step + 1) * HIDDEN, :])
        tend = tend.astype(BF16).astype(F32)
        if step == 0:
            fetch.wait()
        for k in range(GROUP):
            here = pl.ds(GROUP * step + k, FEATURES, stride=ROWS)
            lines[here, :] = lines[here, :] + tend[:, k * COLS : (k + 1) * COLS]
    first = pltpu.make_async_copy(mixed, out.at[:, pl.ds(0, SLICE), :], sems.at[batches])
    first.start()
    copies = [
        pltpu.make_async_copy(
            held.at[pl.ds(1 + n * BATCH, BATCH)],
            out.at[pl.ds(n * BATCH, BATCH), pl.ds(SLICE, SLICE), :],
            sems.at[n],
        )
        for n in range(batches)
    ]
    advance(KINDS, ins, lambda: None, lambda n: copies[n].start(), scratch)
    first.wait()
    for copy in copies:
        copy.wait()


def run(kernel, outs, scratch, flops, moved, *args, name=None, far=(), limit=58 * 1024 * 1024, **rest):
    anywhere, near = pl.BlockSpec(memory_space=pl.ANY), pl.BlockSpec(memory_space=pltpu.VMEM)
    rest = rest or dict(in_specs=[anywhere if n in far else near for n in range(len(args))])
    return pl.pallas_call(
        kernel,
        out_shape=[jax.ShapeDtypeStruct(shape, kind) for shape, kind in outs],
        scratch_shapes=scratch,
        compiler_params=pltpu.CompilerParams(vmem_limit_bytes=limit),
        cost_estimate=pl.CostEstimate(flops=flops, bytes_accessed=moved, transcendentals=0),
        name=name,
        **rest,
    )(*args)


FAR = (0, 1, 2, 3)


def main(ins, cotan, *weights):
    near = pl.BlockSpec(memory_space=pltpu.VMEM)
    far = pl.BlockSpec(memory_space=pl.ANY)
    outs = [
        ((LEVELS, SLICE, COLS), F32),
        ((ROWS * COLS, FEATURES), BF16),
        ((ROWS // GROUP * HIDDEN, GROUP * COLS), BF16),
    ]
    held = [pltpu.VMEM(x.shape, BF16) for x in (cotan,) + weights]
    held += [pltpu.VMEM(*outs[1]), pltpu.VMEM(*outs[2]), pltpu.SemaphoreType.DMA((10 + 2 * ROWS // GROUP,))]
    return run(
        main_kernel, outs, held + advance_scratch(), 4 * 10**9, 10**7, *ins, cotan, *weights, name="main",
        in_specs=[far if n in FAR or n >= 9 else near for n in range(15)], out_specs=[far] * 3,
    )


def last(ins, solved, active, w_out_t):
    near = pl.BlockSpec(memory_space=pltpu.VMEM)
    far = pl.BlockSpec(memory_space=pl.ANY)
    mixed = [pltpu.VMEM((LEVELS, SLICE, COLS), F32), pltpu.SemaphoreType.DMA((LEVELS // BATCH + 2,))]
    (new_state,) = run(
        last_kernel, [((LEVELS, FIELDS * ROWS, COLS), F32)], mixed + advance_scratch(), 10**9, 2 * 10**7,
        *ins, solved, active, w_out_t, name="last_fields",
        in_specs=[far if n in FAR + (9,) else near for n in range(12)], out_specs=[far],
    )
    return new_state


def swap(block, axis, start):
    firsts = range(start, lax.axis_size(axis) - 1, 2)
    return lax.ppermute(block, axis, [(i, i + 1) for i in firsts] + [(i + 1, i) for i in firsts])


def exchange(blocks):
    return lax.all_to_all(blocks, ("gx", "gy"), split_axis=0, concat_axis=0, tiled=True)


def shards(state, east_wind, north_wind, kappa, w_in, w_mid, w_out, cotangent):
    devices = lax.axis_size("gx") * lax.axis_size("gy")
    flat = state.reshape(LEVELS * FIELDS * ROWS, COLS)
    east = east_wind.reshape(LEVELS * ROWS, COLS)
    north = north_wind.reshape(LEVELS * ROWS, COLS)
    message = ((ROW_MESSAGE, COLS), BF16)
    to_partner, to_other = run(rows_kernel, [message, message], [], 10**6, 5 * 10**6, flat, east, north, name="rows")
    arrived = exchange(cotangent.reshape(devices, ROWS * COLS // devices, FEATURES))
    from_other = swap(to_other, "gx", 1)
    from_partner = swap(to_partner, "gx", 0)
    count = LEVELS * FIELDS
    flipped = [(w.shape[::-1], BF16) for w in (w_in, w_mid, w_out)]
    edges, w_in_t, w_mid_t, w_out_t = run(
        cols_kernel, [((COL_MESSAGE - 48, COLS), BF16)] + flipped, [], 10**8, 10**7,
        flat, east, north, w_in, w_mid, w_out, name="cols",
    )
    (own,) = run(
        corners_kernel, [((COL_MESSAGE, COLS), BF16)], [pltpu.VMEM((count, COLS), BF16)], 10**6, 10**6,
        edges, from_partner, from_other, name="corners", limit=8 * 1024 * 1024,
    )
    rows_partner, rows_other = from_partner, from_other
    from_other = swap(own, "gy", 1)
    from_partner = swap(own, "gy", 0)
    ins = (state.reshape(LEVELS, FIELDS * ROWS, COLS), east, north, kappa.reshape((LEVELS - 1) * ROWS, COLS))
    ins += (rows_partner, rows_other, own, from_partner, from_other)
    cotan = arrived.reshape(ROWS * COLS, FEATURES)
    solved, adjoint, active = main(ins, cotan, w_in_t, w_mid_t, w_out, w_mid, w_in)
    returned = exchange(adjoint.reshape(devices, ROWS * COLS // devices, FEATURES))
    new_state = last(ins, solved, active, w_out_t)
    return new_state.reshape(state.shape), returned.reshape(ROWS * COLS, FEATURES)


def solution(mesh):
    in_specs = (
        P(None, None, "gx", "gy"),
        P(None, "gx", "gy"),
        P(None, "gx", "gy"),
        P(None, "gx", "gy"),
        P(),
        P(),
        P(),
        P(("gx", "gy"), None),
    )
    out_specs = (P(None, None, "gx", "gy"), P(("gx", "gy"), None))
    return jax.shard_map(shards, mesh=mesh, in_specs=in_specs, out_specs=out_specs, check_vma=False)
```
